256 devices in a mesh: batch: 2 (over y_hi), tm: 16 (over z, y_lo), height: 8 (over x, core).
Axes of the slice: x: 4, y: 4 (y_hi: 2, y_lo: 2; y = y_hi * 2 + y_lo), z: 8, core: 2. Of those that a mesh axis runs over, the one named last changes fastest.
Arguments:
- features: bfloat16 [2, 32, 64, 128, 128], P('batch', 'tm', 'height'), may hold values from -6 to 6
- w_spatial: bfloat16 [3, 3, 128, 128], replicated, may hold values from -0.1875 to 0.1875
- w_temporal: bfloat16 [3, 128, 128], replicated, may hold values from -0.3125 to 0.3125
- w_down: bfloat16 [3, 128, 128], replicated, may hold values from -0.3125 to 0.3125
- cotangent: bfloat16 [2, 16, 64, 128, 128], P('batch', 'tm', 'height'), may hold values from -40 to 40
Outputs:
- downsampled: bfloat16 [2, 16, 64, 128, 128], P('batch', 'tm', 'height')
- grad_features: bfloat16 [2, 32, 64, 128, 128], P('batch', 'tm', 'height')
- grad_spatial: float32 [3, 3, 128, 128], replicated
- grad_temporal: float32 [3, 128, 128], replicated
- grad_down: float32 [3, 128, 128], replicated
The draws below stay inside these ranges and needn't reach their ends.
All inputs are finite; a program needn't handle non-finite values.
Results may differ from the reference program's by a relative error of at most 0.0052.
Values may be sent and summed in bfloat16 or wider, within the bound.
No kernel may reach another device: no remote copies, remote signals or barrier semaphores. Data moves between devices by JAX's collectives and lax.ppermute only.
A program may use at most 64 MiB of HBM per device.

```python
import jax
import jax.numpy as jnp

C = 128
WIDTH = 128
CLIPS = 2
FRAMES = 32
HEIGHT = 64


def draw_cotangent(key, part):
    key = jax.random.fold_in(key, 7)
    shape = (CLIPS, FRAMES // 2, HEIGHT, WIDTH, C)
    first = jax.random.fold_in(key, 0)
    third = jax.random.fold_in(key, 2)
    frame_pos = jnp.arange(FRAMES // 2, dtype=jnp.float32) / max(FRAMES // 2 - 1, 1)
    row_pos = jnp.arange(HEIGHT, dtype=jnp.float32) / max(HEIGHT - 1, 1)
    scale = jnp.exp(jnp.log(3.0) * frame_pos)[None, :, None, None, None] * jnp.exp(jnp.log(3.0) * row_pos)[None, None, :, None, None]
    chan = jnp.exp(jax.random.uniform(third, (C,), jnp.float32, 0.0, jnp.log(4.0)))
    values = jnp.clip(jax.random.normal(first, shape, jnp.float32), -4.0, 4.0) * scale * chan
    return jnp.clip(values, -40.0, 40.0).astype(jnp.bfloat16)


def shard_levels(rng, shape, cuts, least, top_value):
    level, own = 1.0, jax.random.fold_in(rng, 6)
    for dim, parts in cuts:
        draws = jnp.exp(jax.random.uniform(jax.random.fold_in(own, dim), (parts,), jnp.float32, least / len(cuts), top_value / len(cuts)))
        level = level * jnp.repeat(draws, shape[dim] // parts).reshape([-1 if axis == dim else 1 for axis in range(len(shape))])
    return level


def bell_draw(stream_key, dims, deviation, most, cuts=(), kind=jnp.bfloat16):
    drawn = jax.random.normal(stream_key, dims, jnp.float32) * deviation
    if len(cuts) > 0:
        drawn = shard_levels(stream_key, dims, cuts, -0.22, 0.18) * drawn
    return jnp.clip(drawn, min=-most, max=most).astype(kind)


def setup_inputs(seed: int = 0) -> dict:
    key_list = jax.random.split(jax.random.key(seed), 6)
    return {
        "features": bell_draw(key_list[0], (CLIPS, FRAMES, HEIGHT, WIDTH, C), 1.0, 6.0, ((0, 2), (1, 16), (2, 8))),
        "w_spatial": bell_draw(key_list[1], (3, 3, C, C), (9 * C) ** -0.5, 0.1875),
        "w_temporal": bell_draw(key_list[2], (3, C, C), (3 * C) ** -0.5, 0.3125),
        "w_down": bell_draw(key_list[3], (3, C, C), (3 * C) ** -0.5, 0.3125),
        "cotangent": draw_cotangent(jax.random.fold_in(key_list[5], 71), 0),
    }


def spatial(padded, kernel):
    rows = padded.shape[2] - 2
    cols = padded.shape[3]
    wide = jnp.pad(padded, ((0, 0), (0, 0), (0, 0), (1, 1), (0, 0))).astype(jnp.float32)
    kern = kernel.astype(jnp.float32)
    total = jnp.zeros(padded.shape[:2] + (rows, cols, kernel.shape[3]), jnp.float32)
    for dy in range(3):
        for dx in range(3):
            total = total + jnp.einsum('bfhwc,cd->bfhwd', wide[:, :, dy:dy + rows, dx:dx + cols], kern[dy, dx])
    return total

def spatial_grad(padded, grad):
    rows = grad.shape[2]
    cols = grad.shape[3]
    wide = jnp.pad(padded, ((0, 0), (0, 0), (0, 0), (1, 1), (0, 0))).astype(jnp.float32)
    gfl = grad.astype(jnp.float32)
    taps = []
    for dy in range(3):
        for dx in range(3):
            taps.append(jnp.einsum('bfhwc,bfhwd->cd', wide[:, :, dy:dy + rows, dx:dx + cols], gfl))
    return jnp.stack(taps).reshape(3, 3, grad.shape[4], grad.shape[4])

def temporal(padded, kernel):
    frames = padded.shape[1] - 2
    pfl = padded.astype(jnp.float32)
    kern = kernel.astype(jnp.float32)
    total = jnp.zeros(padded.shape[:1] + (frames,) + padded.shape[2:4] + (kernel.shape[2],), jnp.float32)
    for k in range(3):
        total = total + jnp.einsum('bfhwc,cd->bfhwd', pfl[:, k:k + frames], kern[k])
    return total

def reference(features, w_spatial, w_temporal, w_down, cotangent):
    frames = features.shape[1]
    half = frames // 2
    rowpad = ((0, 0), (0, 0), (1, 1), (0, 0), (0, 0))
    framepad = ((0, 0), (1, 1), (0, 0), (0, 0), (0, 0))
    xpad = jnp.pad(features, rowpad)
    pre = spatial(xpad, w_spatial)
    act = jax.nn.silu(pre).astype(jnp.bfloat16)
    act_pad = jnp.pad(act, framepad)
    mixed = temporal(act_pad, w_temporal)
    resid = (features.astype(jnp.float32) + mixed).astype(jnp.bfloat16)
    rpad = jnp.pad(resid, ((0, 0), (1, 0), (0, 0), (0, 0), (0, 0))).astype(jnp.float32)
    wd = w_down.astype(jnp.float32)
    gfl = cotangent.astype(jnp.float32)
    down = jnp.zeros(cotangent.shape, jnp.float32)
    grad_down = []
    for k in range(3):
        picked = rpad[:, k:k + 2 * half:2]
        down = down + jnp.einsum('bfhwc,cd->bfhwd', picked, wd[k])
        grad_down.append(jnp.einsum('bfhwc,bfhwd->cd', picked, gfl))
    grad_down = jnp.stack(grad_down)
    downsampled = down.astype(jnp.bfloat16)
    gnext = jnp.concatenate([gfl[:, 1:], jnp.zeros_like(gfl[:, :1])], axis=1)
    even = jnp.einsum('bfhwd,cd->bfhwc', gfl, wd[1])
    odd = jnp.einsum('bfhwd,cd->bfhwc', gfl, wd[2]) + jnp.einsum('bfhwd,cd->bfhwc', gnext, wd[0])
    g_resid = jnp.stack([even, odd], axis=2).reshape(features.shape)
    g_resid_b = g_resid.astype(jnp.bfloat16)
    flip_t = jnp.transpose(w_temporal[::-1], (0, 2, 1))
    g_act = temporal(jnp.pad(g_resid_b, framepad), flip_t)
    gr_fl = g_resid_b.astype(jnp.float32)
    apf = act_pad.astype(jnp.float32)
    grad_temporal = jnp.stack([jnp.einsum('bfhwc,bfhwd->cd', apf[:, k:k + frames], gr_fl) for k in range(3)])
    sig = jax.nn.sigmoid(pre)
    g_pre = (g_act * sig * (1.0 + pre * (1.0 - sig))).astype(jnp.bfloat16)
    grad_spatial = spatial_grad(xpad, g_pre)
    flip_s = jnp.transpose(w_spatial[::-1, ::-1], (0, 1, 3, 2))
    grad_features = (g_resid + spatial(jnp.pad(g_pre, rowpad), flip_s)).astype(jnp.bfloat16)
    return (downsampled, grad_features, grad_spatial, grad_temporal, grad_down)
```

```python
import jax
import jax.numpy as jnp
from jax import lax
from jax.experimental import pallas as pl
from jax.experimental.pallas import tpu as pltpu
from jax.sharding import Mesh, PartitionSpec as P

F32, BF16 = jnp.float32, jnp.bfloat16
C = 128
PLANE = ("yh", "yl", "x")


def mm(a, b):
    return lax.dot_general(a, b, (((1,), (0,)), ((), ())), preferred_element_type=F32)


def mm_nt(a, b):
    return lax.dot_general(a, b, (((1,), (1,)), ((), ())), preferred_element_type=F32)


def mm_tn(a, b):
    return lax.dot_general(a, b, (((0,), (0,)), ((), ())), preferred_element_type=F32)


def columns(x):
    wide = x.astype(F32)
    count = wide.shape[0]
    col = lax.broadcasted_iota(jnp.int32, wide.shape, 0) % 128
    before = jnp.where(col == 0, 0.0, pltpu.roll(wide, 1, 0)).astype(BF16)
    after = jnp.where(col == 127, 0.0, pltpu.roll(wide, count - 1, 0)).astype(BF16)
    return before, x, after


def row_pairs(cat):
    depth = cat.shape[1]
    rows = cat.reshape(5, 2, 128, depth)
    even, odd = rows[:, 0], rows[:, 1]
    parts = [even[0:4], odd[0:4], even[1:5], odd[1:5]]
    return jnp.concatenate([p.reshape(512, depth) for p in parts], axis=1)


def forward_kernel(x_ref, lo_ref, hi_ref, w_ref, slope_ref, act_ref, xt_ref, at_ref, wide_ref):
    wide_ref[...] = jnp.zeros_like(wide_ref)
    for out in range(2):
        for dy in range(3):
            for dx in range(3):
                start = ((dy + out) * 3 + dx) * C
                wide_ref[start : start + C, out * C : (out + 1) * C] = w_ref[dy, dx]
    for f in range(2):
        x = jnp.concatenate([lo_ref[f], x_ref[f], hi_ref[f]], axis=0).reshape(1280, C)
        xt_ref[f] = x.T
        pre = mm(row_pairs(jnp.concatenate(columns(x), axis=1)), wide_ref[...])
        sig = 1.0 / (1.0 + jnp.exp(-pre))
        act = (pre * sig).astype(BF16)
        slope = sig * (1.0 + pre * (1.0 - sig))
        for out in range(2):
            part = slice(out * C, (out + 1) * C)
            act_ref[f, :, out] = act[:, part].reshape(4, 128, C)
            slope_ref[f, :, out] = slope[:, part].reshape(4, 128, C)
        at_ref[f] = act_ref[f].reshape(1024, C).T


def grads_kernel(
    place_ref, slope_ref, xt_ref, at_ref, cot_ref, prev_ref, next_ref, wt_ref, wd_ref,
    gpre_ref, send_ref, keep_ref, mats_ref,
):
    first = place_ref[0] == 0
    core = place_ref[1]
    cot, before, after = (r[...].reshape(1024, C) for r in (cot_ref, prev_ref, next_ref))
    zero = jnp.zeros((C, C), BF16)
    w_pair = jnp.concatenate(
        [
            jnp.concatenate([wd_ref[2], wd_ref[0]], axis=1),
            jnp.concatenate([zero, wd_ref[1]], axis=1),
        ],
        axis=0,
    )
    low = mm_nt(jnp.concatenate([before, cot], axis=1), w_pair).astype(BF16)
    high = mm_nt(jnp.concatenate([cot, after], axis=1), w_pair).astype(BF16)
    g_m1 = jnp.where(first, jnp.zeros_like(low[:, :C]), low[:, :C])
    g_0, g_1, g_2 = low[:, C:], high[:, :C], high[:, C:]
    w_time = jnp.concatenate(
        [
            jnp.concatenate([wt_ref[2], wt_ref[1], wt_ref[0], zero], axis=1),
            jnp.concatenate([zero, wt_ref[2], wt_ref[1], wt_ref[0]], axis=1),
        ],
        axis=0,
    )
    g_act = mm_nt(jnp.concatenate([g_m1, g_0, g_1, g_2], axis=1), w_time)
    spatial = None
    for f in range(2):
        gp = (g_act[:, f * C : (f + 1) * C] * slope_ref[f].reshape(1024, C)).astype(BF16)
        gpre_ref[f] = gp.reshape(8, 128, C)
        behind, here, ahead = columns(gp)
        shifted = jnp.concatenate([ahead, here, behind], axis=1)
        xt = jnp.concatenate([xt_ref[f, :, dy * 128 : dy * 128 + 1024] for dy in range(3)], axis=0)
        term = mm(xt, shifted)
        spatial = term if spatial is None else spatial + term
    for dy in range(3):
        for dx in range(3):
            mats_ref[dy * 3 + dx] = spatial[dy * C : (dy + 1) * C, dx * C : (dx + 1) * C].reshape(2, 64, C)
    a0, a1 = at_ref[0], at_ref[1]
    x0, x1 = xt_ref[0, :, 128:1152], xt_ref[1, :, 128:1152]
    time = mm(a0, jnp.concatenate([g_1, g_0, g_m1], axis=1))
    time = time + mm(a1, jnp.concatenate([g_2, g_1, g_0], axis=1))
    for k in range(3):
        mats_ref[9 + k] = time[:, k * C : (k + 1) * C].reshape(2, 64, C)
    both = mm(
        jnp.concatenate([a0, a1, x0, x1], axis=0), jnp.concatenate([cot, after], axis=1)
    )
    tail = mm(a0, before)
    m_0, m_1 = both[0:128, :C], both[128:256, :C]
    m_m2, m_m1 = both[0:128, C:], both[128:256, C:]
    skip = jnp.where(first, jnp.zeros_like(m_0), m_0)
    kinds = (
        (both[384:512, C:], (m_m2, m_m1, skip)),
        (both[256:384, :C], (m_m1, m_0, m_1)),
        (both[384:512, :C], (m_0, m_1, tail)),
    )
    for k, (base, terms) in enumerate(kinds):
        total = base
        for tap, m in enumerate(terms):
            top = m.astype(BF16)
            rest = (m - top.astype(F32)).astype(BF16)
            total = total + mm_tn(wt_ref[tap], top) + mm_tn(wt_ref[tap], rest)
        mats_ref[12 + k] = total.reshape(2, 64, C)
    send_ref[...] = mats_ref[:, 1 - core].astype(BF16)
    keep_ref[...] = mats_ref[:, core]


def resid_kernel(x_ref, act_ref, prev_ref, next_ref, wt_ref, resid_ref):
    zero = jnp.zeros((C, C), BF16)
    w_time = jnp.concatenate(
        [
            jnp.concatenate([wt_ref[0], wt_ref[1], wt_ref[2], zero], axis=0),
            jnp.concatenate([zero, wt_ref[0], wt_ref[1], wt_ref[2]], axis=0),
        ],
        axis=1,
    )
    parts = [prev_ref[...], act_ref[0], act_ref[1], next_ref[...]]
    mixed = mm(jnp.concatenate([p.reshape(1024, C) for p in parts], axis=1), w_time)
    for f in range(2):
        total = x_ref[f].astype(F32).reshape(1024, C) + mixed[:, f * C : (f + 1) * C]
        resid_ref[f] = total.astype(BF16).reshape(8, 128, C)


def down_kernel(resid_ref, before_ref, wd_ref, out_ref):
    parts = [before_ref[...], resid_ref[0], resid_ref[1]]
    rows = jnp.concatenate([p.reshape(1024, C) for p in parts], axis=1)
    weights = jnp.concatenate([wd_ref[0], wd_ref[1], wd_ref[2]], axis=0)
    out_ref[...] = mm(rows, weights).astype(BF16).reshape(8, 128, C)


def features_kernel(gpre_ref, lo_ref, hi_ref, cot_ref, next_ref, w_ref, wd_ref, out_ref, wide_ref):
    wide_ref[...] = jnp.zeros_like(wide_ref)
    for out in range(2):
        for dy in range(3):
            for dx in range(3):
                start = ((dy + out) * 3 + dx) * C
                wide_ref[out * C : (out + 1) * C, start : start + C] = w_ref[2 - dy, 2 - dx]
    zero = jnp.zeros((C, C), BF16)
    w_pair = jnp.concatenate(
        [
            jnp.concatenate([wd_ref[1], zero], axis=1),
            jnp.concatenate([wd_ref[2], wd_ref[0]], axis=1),
        ],
        axis=0,
    )
    cot, after = (r[...].reshape(1024, C) for r in (cot_ref, next_ref))
    resid = mm_nt(jnp.concatenate([cot, after], axis=1), w_pair)
    for f in range(2):
        g = jnp.concatenate([lo_ref[f], gpre_ref[f], hi_ref[f]], axis=0).reshape(1280, C)
        conv = mm_nt(row_pairs(jnp.concatenate(columns(g), axis=1)), wide_ref[...])
        base = resid[:, f * C : (f + 1) * C].reshape(4, 2, 128, C)
        for out in range(2):
            part = conv[:, out * C : (out + 1) * C].reshape(4, 128, C)
            out_ref[f, :, out] = (base[:, out] + part).astype(BF16)


VMEM = pl.BlockSpec(memory_space=pltpu.VMEM)
SMEM = pl.BlockSpec(memory_space=pltpu.SMEM)


def call(kernel, outs, args, taps, scratch=(), scalars=0):
    return pl.pallas_call(
        kernel,
        out_shape=[jax.ShapeDtypeStruct(s, d) for s, d in outs],
        in_specs=[SMEM] * scalars + [VMEM] * (len(args) - scalars),
        out_specs=[VMEM] * len(outs),
        scratch_shapes=list(scratch),
        compiler_params=pltpu.CompilerParams(vmem_limit_bytes=40 * 1024 * 1024),
        cost_estimate=pl.CostEstimate(
            flops=int(taps * 2048 * C * C * 2), bytes_accessed=4_000_000, transcendentals=0
        ),
    )(*args)


def shift(x, axis, by):
    count = lax.axis_size(axis)
    return lax.ppermute(x, axis, [(i, i + by) for i in range(count) if 0 <= i + by < count])


def swap(x, axis, mask):
    return lax.ppermute(x, axis, [(i, i ^ mask) for i in range(lax.axis_size(axis))])


def sum_all(send, keep, core):
    half = keep + swap(send, "core", 1).astype(F32)
    half = jnp.concatenate([half.astype(BF16), jnp.zeros((1, 64, C), BF16)])
    got = lax.all_to_all(half, PLANE, 0, 0, tiled=True)
    total = jnp.sum(got.astype(F32), axis=0)
    for mask in (1, 2, 4):
        total = total + swap(total, "z", mask)
    out = jnp.broadcast_to(total.astype(BF16), (16, 64, C))
    out = lax.all_to_all(out, PLANE, 0, 0, tiled=True)[:15]
    other = swap(out, "core", 1)
    low, high = jnp.where(core == 0, out, other), jnp.where(core == 0, other, out)
    return jnp.concatenate([low, high], axis=1).astype(F32)


def per_device(features, w_spatial, w_temporal, w_down, cotangent):
    time, rows = ("z", "yl"), ("x", "core")
    x, cot = features[0], cotangent[0, 0]
    core = lax.axis_index("core")
    place = jnp.stack([lax.axis_index(time), core]).astype(jnp.int32)
    lo, hi = shift(x[:, 7:], rows, 1), shift(x[:, :1], rows, -1)
    cot_prev, cot_next = shift(cot, time, 1), shift(cot, time, -1)
    slope, act, xt, at = call(
        forward_kernel,
        [((2, 4, 2, 128, C), F32), ((2, 4, 2, 128, C), BF16), ((2, C, 1280), BF16), ((2, C, 1024), BF16)],
        (x, lo, hi, w_spatial), 9,
        scratch=[pltpu.VMEM((12 * C, 2 * C), BF16)],
    )
    gpre, send, keep = call(
        grads_kernel,
        [((2, 8, 128, C), BF16), ((15, 64, C), BF16), ((15, 64, C), F32)],
        (place, slope, xt, at, cot, cot_prev, cot_next, w_temporal, w_down), 21,
        scratch=[pltpu.VMEM((15, 2, 64, C), F32)], scalars=1,
    )
    grads = sum_all(send, keep, core)
    act = act.reshape(2, 8, 128, C)
    act_prev, act_next = shift(act[1], time, 1), shift(act[0], time, -1)
    g_lo, g_hi = shift(gpre[:, 7:], rows, 1), shift(gpre[:, :1], rows, -1)
    (resid,) = call(
        resid_kernel, [((2, 8, 128, C), BF16)], (x, act, act_prev, act_next, w_temporal), 3
    )
    before = shift(resid[1], time, 1)
    (grad_features,) = call(
        features_kernel, [((2, 4, 2, 128, C), BF16)],
        (gpre, g_lo, g_hi, cot, cot_next, w_spatial, w_down), 11,
        scratch=[pltpu.VMEM((2 * C, 12 * C), BF16)],
    )
    (down,) = call(down_kernel, [((8, 128, C), BF16)], (resid, before, w_down), 1.5)
    return (
        down[None, None],
        grad_features.reshape(1, 2, 8, 128, C),
        grads[:9].reshape(3, 3, C, C),
        grads[9:12],
        grads[12:],
    )


def solution(mesh):
    fine = Mesh(mesh.devices.reshape(2, 8, 2, 4, 2), ("yh", "z", "yl", "x", "core"))
    block = P("yh", ("z", "yl"), ("x", "core"), None, None)
    return jax.shard_map(
        per_device,
        mesh=fine,
        in_specs=(block, P(), P(), P(), block),
        out_specs=(block, block, P(), P(), P()),
        check_vma=False,
    )
```

```python
import jax
import jax.numpy as jnp
from jax import lax
from jax.experimental import pallas as pl
from jax.experimental.pallas import tpu as pltpu
from jax.sharding import Mesh, PartitionSpec as P

F32, BF16 = jnp.float32, jnp.bfloat16
C = 128
PLANE = ("yh", "yl", "x")


def mm(a, b):
    return lax.dot_general(a, b, (((1,), (0,)), ((), ())), preferred_element_type=F32)


def mm_nt(a, b):
    return lax.dot_general(a, b, (((1,), (1,)), ((), ())), preferred_element_type=F32)


def mm_tn(a, b):
    return lax.dot_general(a, b, (((0,), (0,)), ((), ())), preferred_element_type=F32)


def columns(x):
    wide = x.astype(F32)
    count = wide.shape[0]
    col = lax.broadcasted_iota(jnp.int32, wide.shape, 0) % 128
    before = jnp.where(col == 0, 0.0, pltpu.roll(wide, 1, 0)).astype(BF16)
    after = jnp.where(col == 127, 0.0, pltpu.roll(wide, count - 1, 0)).astype(BF16)
    return before, x, after


def row_pairs(cat):
    depth = cat.shape[1]
    rows = cat.reshape(5, 2, 128, depth)
    even, odd = rows[:, 0], rows[:, 1]
    parts = [even[0:4], odd[0:4], even[1:5], odd[1:5]]
    return jnp.concatenate([p.reshape(512, depth) for p in parts], axis=1)


def sides(place_ref, at, near, far):
    odd = place_ref[at] % 2 == 1
    return jnp.where(odd, near, far), jnp.where(odd, far, near)


def forward_kernel(
    place_ref, x_ref, near_ref, far_ref, w_ref, slope_ref, act_ref, xt_ref, at_ref, wide_ref
):
    wide_ref[...] = jnp.zeros_like(wide_ref)
    for out in range(2):
        for dy in range(3):
            for dx in range(3):
                start = ((dy + out) * 3 + dx) * C
                wide_ref[start : start + C, out * C : (out + 1) * C] = w_ref[dy, dx]
    for f in range(2):
        lo, hi = sides(place_ref, 1, near_ref[f], far_ref[f])
        x = jnp.concatenate([lo[None], x_ref[f], hi[None]], axis=0).reshape(1280, C)
        xt_ref[f] = x.T
        pre = mm(row_pairs(jnp.concatenate(columns(x), axis=1)), wide_ref[...])
        sig = 1.0 / (1.0 + jnp.exp(-pre))
        act = (pre * sig).astype(BF16)
        slope = sig * (1.0 + pre * (1.0 - sig))
        for out in range(2):
            part = slice(out * C, (out + 1) * C)
            act_ref[f, :, out] = act[:, part].reshape(4, 128, C)
            slope_ref[f, :, out] = slope[:, part].reshape(4, 128, C)
        at_ref[f] = act_ref[f].reshape(1024, C).T


def grads_kernel(
    place_ref, slope_ref, xt_ref, at_ref, cot_ref, near_ref, far_ref, wt_ref, wd_ref,
    gpre_ref, send_ref, keep_ref, mats_ref,
):
    first = place_ref[0] == 0
    core = place_ref[1]
    cot, near, far = (r[...].reshape(1024, C) for r in (cot_ref, near_ref, far_ref))
    before, after = sides(place_ref, 0, near, far)
    zero = jnp.zeros((C, C), BF16)
    w_pair = jnp.concatenate(
        [
            jnp.concatenate([wd_ref[2], wd_ref[0]], axis=1),
            jnp.concatenate([zero, wd_ref[1]], axis=1),
        ],
        axis=0,
    )
    low = mm_nt(jnp.concatenate([before, cot], axis=1), w_pair).astype(BF16)
    high = mm_nt(jnp.concatenate([cot, after], axis=1), w_pair).astype(BF16)
    g_m1 = jnp.where(first, jnp.zeros_like(low[:, :C]), low[:, :C])
    g_0, g_1, g_2 = low[:, C:], high[:, :C], high[:, C:]
    w_time = jnp.concatenate(
        [
            jnp.concatenate([wt_ref[2], wt_ref[1], wt_ref[0], zero], axis=1),
            jnp.concatenate([zero, wt_ref[2], wt_ref[1], wt_ref[0]], axis=1),
        ],
        axis=0,
    )
    g_act = mm_nt(jnp.concatenate([g_m1, g_0, g_1, g_2], axis=1), w_time)
    spatial = None
    for f in range(2):
        gp = (g_act[:, f * C : (f + 1) * C] * slope_ref[f].reshape(1024, C)).astype(BF16)
        gpre_ref[f] = gp.reshape(8, 128, C)
        behind, here, ahead = columns(gp)
        shifted = jnp.concatenate([ahead, here, behind], axis=1)
        xt = jnp.concatenate([xt_ref[f, :, dy * 128 : dy * 128 + 1024] for dy in range(3)], axis=0)
        term = mm(xt, shifted)
        spatial = term if spatial is None else spatial + term
    for dy in range(3):
        for dx in range(3):
            mats_ref[dy * 3 + dx] = spatial[dy * C : (dy + 1) * C, dx * C : (dx + 1) * C].reshape(2, 64, C)
    a0, a1 = at_ref[0], at_ref[1]
    x0, x1 = xt_ref[0, :, 128:1152], xt_ref[1, :, 128:1152]
    time = mm(a0, jnp.concatenate([g_1, g_0, g_m1], axis=1))
    time = time + mm(a1, jnp.concatenate([g_2, g_1, g_0], axis=1))
    for k in range(3):
        mats_ref[9 + k] = time[:, k * C : (k + 1) * C].reshape(2, 64, C)
    both = mm(
        jnp.concatenate([a0, a1, x0, x1], axis=0), jnp.concatenate([cot, after], axis=1)
    )
    tail = mm(a0, before)
    m_0, m_1 = both[0:128, :C], both[128:256, :C]
    m_m2, m_m1 = both[0:128, C:], both[128:256, C:]
    skip = jnp.where(first, jnp.zeros_like(m_0), m_0)
    kinds = (
        (both[384:512, C:], (m_m2, m_m1, skip)),
        (both[256:384, :C], (m_m1, m_0, m_1)),
        (both[384:512, :C], (m_0, m_1, tail)),
    )
    for k, (base, terms) in enumerate(kinds):
        total = base
        for tap, m in enumerate(terms):
            top = m.astype(BF16)
            rest = (m - top.astype(F32)).astype(BF16)
            total = total + mm_tn(wt_ref[tap], top) + mm_tn(wt_ref[tap], rest)
        mats_ref[12 + k] = total.reshape(2, 64, C)
    send_ref[...] = mats_ref[:, 1 - core].astype(BF16)
    keep_ref[...] = mats_ref[:, core]


def resid_kernel(place_ref, x_ref, act_ref, near_ref, far_ref, wt_ref, resid_ref):
    zero = jnp.zeros((C, C), BF16)
    w_time = jnp.concatenate(
        [
            jnp.concatenate([wt_ref[0], wt_ref[1], wt_ref[2], zero], axis=0),
            jnp.concatenate([zero, wt_ref[0], wt_ref[1], wt_ref[2]], axis=0),
        ],
        axis=1,
    )
    parts = [r.reshape(1024, C) for r in (near_ref[...], far_ref[...], act_ref[0], act_ref[1])]
    before, after = sides(place_ref, 0, parts[0], parts[1])
    mixed = mm(jnp.concatenate([before, parts[2], parts[3], after], axis=1), w_time)
    for f in range(2):
        total = x_ref[f].astype(F32).reshape(1024, C) + mixed[:, f * C : (f + 1) * C]
        resid_ref[f] = total.astype(BF16).reshape(8, 128, C)


def down_kernel(resid_ref, before_ref, wd_ref, out_ref):
    parts = [before_ref[...], resid_ref[0], resid_ref[1]]
    rows = jnp.concatenate([p.reshape(1024, C) for p in parts], axis=1)
    weights = jnp.concatenate([wd_ref[0], wd_ref[1], wd_ref[2]], axis=0)
    out_ref[...] = mm(rows, weights).astype(BF16).reshape(8, 128, C)


def features_kernel(
    place_ref, gpre_ref, g_near_ref, g_far_ref, cot_ref, near_ref, far_ref, w_ref, wd_ref,
    out_ref, wide_ref,
):
    wide_ref[...] = jnp.zeros_like(wide_ref)
    for out in range(2):
        for dy in range(3):
            for dx in range(3):
                start = ((dy + out) * 3 + dx) * C
                wide_ref[out * C : (out + 1) * C, start : start + C] = w_ref[2 - dy, 2 - dx]
    zero = jnp.zeros((C, C), BF16)
    w_pair = jnp.concatenate(
        [
            jnp.concatenate([wd_ref[1], zero], axis=1),
            jnp.concatenate([wd_ref[2], wd_ref[0]], axis=1),
        ],
        axis=0,
    )
    cot, near, far = (r[...].reshape(1024, C) for r in (cot_ref, near_ref, far_ref))
    after = sides(place_ref, 0, near, far)[1]
    resid = mm_nt(jnp.concatenate([cot, after], axis=1), w_pair)
    for f in range(2):
        lo, hi = sides(place_ref, 1, g_near_ref[f], g_far_ref[f])
        g = jnp.concatenate([lo[None], gpre_ref[f], hi[None]], axis=0).reshape(1280, C)
        conv = mm_nt(row_pairs(jnp.concatenate(columns(g), axis=1)), wide_ref[...])
        base = resid[:, f * C : (f + 1) * C].reshape(4, 2, 128, C)
        for out in range(2):
            part = conv[:, out * C : (out + 1) * C].reshape(4, 128, C)
            out_ref[f, :, out] = (base[:, out] + part).astype(BF16)


VMEM = pl.BlockSpec(memory_space=pltpu.VMEM)
SMEM = pl.BlockSpec(memory_space=pltpu.SMEM)


def call(kernel, outs, args, taps, scratch=(), scalars=0):
    return pl.pallas_call(
        kernel,
        out_shape=[jax.ShapeDtypeStruct(s, d) for s, d in outs],
        in_specs=[SMEM] * scalars + [VMEM] * (len(args) - scalars),
        out_specs=[VMEM] * len(outs),
        scratch_shapes=list(scratch),
        compiler_params=pltpu.CompilerParams(vmem_limit_bytes=40 * 1024 * 1024),
        cost_estimate=pl.CostEstimate(
            flops=int(taps * 2048 * C * C * 2), bytes_accessed=4_000_000, transcendentals=0
        ),
    )(*args)


def gather_kernel(place_ref, mine_ref, other_ref, spatial_ref, time_ref, down_ref):
    mine = place_ref[1] == 0
    low = jnp.where(mine, mine_ref[...], other_ref[...]).astype(F32)
    high = jnp.where(mine, other_ref[...], mine_ref[...]).astype(F32)
    for first, ref in ((0, spatial_ref), (9, time_ref), (12, down_ref)):
        count = ref.shape[0]
        ref[:, :64] = low[first : first + count]
        ref[:, 64:] = high[first : first + count]


def shift(x, axis, by):
    count = lax.axis_size(axis)
    return lax.ppermute(x, axis, [(i, i + by) for i in range(count) if 0 <= i + by < count])


def swap(x, axis, mask):
    return lax.ppermute(x, axis, [(i, i ^ mask) for i in range(lax.axis_size(axis))])


def swap_far(x, axis):
    count = lax.axis_size(axis)
    pairs = [(i, i + 1) for i in range(1, count - 1, 2)]
    return lax.ppermute(x, axis, pairs + [(b, a) for a, b in pairs])


def neighbours(low, high, axis):
    odd = lax.axis_index(axis) % 2 == 1
    return swap(jnp.where(odd, low, high), axis, 1), swap_far(jnp.where(odd, high, low), axis)


def per_device(features, w_spatial, w_temporal, w_down, cotangent):
    time, rows = ("z", "yl"), ("x", "core")
    x, cot = features[0], cotangent[0, 0]
    core = lax.axis_index("core")
    place = jnp.stack([lax.axis_index(time), core]).astype(jnp.int32)
    cot_near, cot_far = swap(cot, time, 1), swap_far(cot, time)
    x_near, x_far = neighbours(x[:, 0], x[:, 7], rows)
    slope, act, xt, at = call(
        forward_kernel,
        [((2, 4, 2, 128, C), F32), ((2, 4, 2, 128, C), BF16), ((2, C, 1280), BF16), ((2, C, 1024), BF16)],
        (place, x, x_near, x_far, w_spatial), 9,
        scratch=[pltpu.VMEM((12 * C, 2 * C), BF16)], scalars=1,
    )
    act = act.reshape(2, 8, 128, C)
    act_near, act_far = neighbours(act[0], act[1], time)
    gpre, send, keep = call(
        grads_kernel,
        [((2, 8, 128, C), BF16), ((15, 64, C), BF16), ((15, 64, C), F32)],
        (place, slope, xt, at, cot, cot_near, cot_far, w_temporal, w_down), 21,
        scratch=[pltpu.VMEM((15, 2, 64, C), F32)], scalars=1,
    )
    half = keep + swap(send, "core", 1).astype(F32)
    half = jnp.concatenate([half.astype(BF16), jnp.zeros((1, 64, C), BF16)])
    got = lax.all_to_all(half, PLANE, 0, 0, tiled=True)
    got, act_near, act_far, gpre = lax.optimization_barrier((got, act_near, act_far, gpre))
    total = jnp.sum(got.astype(F32), axis=0)
    total = total + swap(total, "z", 1)
    (resid,) = call(
        resid_kernel, [((2, 8, 128, C), BF16)],
        (place, x, act, act_near, act_far, w_temporal), 3, scalars=1,
    )
    total, resid = lax.optimization_barrier((total, resid))
    before = shift(resid[1], time, 1)
    g_near, g_far = neighbours(gpre[:, 0], gpre[:, 7], rows)
    total = total + swap(total, "z", 2)
    total, g_near, g_far = lax.optimization_barrier((total, g_near, g_far))
    (grad_features,) = call(
        features_kernel, [((2, 4, 2, 128, C), BF16)],
        (place, gpre, g_near, g_far, cot, cot_near, cot_far, w_spatial, w_down), 11,
        scratch=[pltpu.VMEM((2 * C, 12 * C), BF16)], scalars=1,
    )
    total = total + swap(total, "z", 4)
    (down,) = call(down_kernel, [((8, 128, C), BF16)], (resid, before, w_down), 1.5)
    total, grad_features, down = lax.optimization_barrier((total, grad_features, down))
    out = jnp.broadcast_to(total.astype(BF16), (16, 64, C))
    out = lax.all_to_all(out, PLANE, 0, 0, tiled=True)
    grads = call(
        gather_kernel, [((n, C, C), F32) for n in (9, 3, 3)], (place, out, swap(out, "core", 1)), 0,
        scalars=1,
    )
    return (
        down[None, None],
        grad_features.reshape(1, 2, 8, 128, C),
        grads[0].reshape(3, 3, C, C),
        grads[1],
        grads[2],
    )


def solution(mesh):
    fine = Mesh(mesh.devices.reshape(2, 8, 2, 4, 2), ("yh", "z", "yl", "x", "core"))
    block = P("yh", ("z", "yl"), ("x", "core"), None, None)
    return jax.shard_map(
        per_device,
        mesh=fine,
        in_specs=(block, P(), P(), P(), block),
        out_specs=(block, block, P(), P(), P()),
        check_vma=False,
    )
```

```python
import jax
import jax.numpy as jnp
from jax import lax
from jax.experimental import pallas as pl
from jax.experimental.pallas import tpu as pltpu
from jax.sharding import Mesh, PartitionSpec as P

F32, BF16 = jnp.float32, jnp.bfloat16
C = 128
PLANE = ("yh", "yl", "x")


def mm(a, b):
    return lax.dot_general(a, b, (((1,), (0,)), ((), ())), preferred_element_type=F32)


def mm_nt(a, b):
    return lax.dot_general(a, b, (((1,), (1,)), ((), ())), preferred_element_type=F32)


def mm_tn(a, b):
    return lax.dot_general(a, b, (((0,), (0,)), ((), ())), preferred_element_type=F32)


def columns(x):
    wide = x.astype(F32)
    count = wide.shape[0]
    col = lax.broadcasted_iota(jnp.int32, wide.shape, 0) % 128
    before = jnp.where(col == 0, 0.0, pltpu.roll(wide, 1, 0)).astype(BF16)
    after = jnp.where(col == 127, 0.0, pltpu.roll(wide, count - 1, 0)).astype(BF16)
    return before, x, after


def row_pairs(cat):
    depth = cat.shape[1]
    rows = cat.reshape(5, 2, 128, depth)
    even, odd = rows[:, 0], rows[:, 1]
    parts = [even[0:4], odd[0:4], even[1:5], odd[1:5]]
    return jnp.concatenate([p.reshape(512, depth) for p in parts], axis=1)


def frame_index():
    return lax.axis_index("z") * 2 + lax.axis_index("yl")


def sort_sides(odd, near_ref, far_ref, before_ref, after_ref):
    @pl.when(odd)
    def _():
        before_ref[...] = near_ref[...]
        after_ref[...] = far_ref[...]

    @pl.when(jnp.logical_not(odd))
    def _():
        before_ref[...] = far_ref[...]
        after_ref[...] = near_ref[...]


def pick_kernel(low_ref, high_ref, near_ref, far_ref):
    sort_sides(lax.axis_index("core") == 1, low_ref, high_ref, near_ref, far_ref)


def forward_kernel(
    x_ref, near_ref, far_ref, w_ref, wt_ref, wd_ref,
    slope_ref, act_ref, xt_ref, at_ref, to_near_ref, to_far_ref, wide_ref, rows_ref,
):
    wide_ref[...] = jnp.zeros_like(wide_ref)
    for out in range(2):
        for dy in range(3):
            for dx in range(3):
                start = ((dy + out) * 3 + dx) * C
                wide_ref[start : start + C, out * C : (out + 1) * C] = w_ref[dy, dx]
    sort_sides(lax.axis_index("core") == 1, near_ref, far_ref, rows_ref.at[:, 0], rows_ref.at[:, 9])
    rows_ref[:, 1:9] = x_ref[...]
    for f in range(2):
        x = rows_ref[f].reshape(1280, C)
        xt_ref[f] = x.T
        pre = mm(row_pairs(jnp.concatenate(columns(x), axis=1)), wide_ref[...])
        sig = 1.0 / (1.0 + jnp.exp(-pre))
        act = (pre * sig).astype(BF16)
        slope = sig * (1.0 + pre * (1.0 - sig))
        for out in range(2):
            part = slice(out * C, (out + 1) * C)
            act_ref[f, :, out] = act[:, part].reshape(4, 128, C)
            slope_ref[f, :, out] = slope[:, part].reshape(4, 128, C)
        at_ref[f] = act_ref[f].reshape(1024, C).T
    zero = jnp.zeros((C, C), BF16)
    a0, a1 = act_ref[0].reshape(1024, C), act_ref[1].reshape(1024, C)
    w_time = jnp.concatenate(
        [
            jnp.concatenate([wt_ref[0], zero], axis=1),
            jnp.concatenate([wt_ref[1], wt_ref[0]], axis=1),
        ],
        axis=0,
    )
    mixed = mm(jnp.concatenate([a0, a1], axis=1), w_time)
    last = (x_ref[1].reshape(1024, C).astype(F32) + mixed[:, :C]).astype(BF16)
    both = jnp.concatenate([last, mixed[:, C:].astype(BF16)], axis=1)
    ahead = mm(both, jnp.concatenate([wd_ref[0], wd_ref[1]], axis=0)).astype(BF16)
    odd = lax.axis_index("yl") == 1

    @pl.when(odd)
    def _():
        to_near_ref[...] = a0.reshape(8, 128, C)
        to_far_ref[...] = ahead.reshape(8, 128, C)

    @pl.when(jnp.logical_not(odd))
    def _():
        to_near_ref[...] = ahead.reshape(8, 128, C)
        to_far_ref[...] = a0.reshape(8, 128, C)


def grads_kernel(
    slope_ref, xt_ref, at_ref, cot_ref, near_ref, far_ref, wt_ref, wd_ref,
    gpre_ref, to_near_ref, to_far_ref, send_ref, keep_ref, mats_ref, before_ref, after_ref,
):
    first = frame_index() == 0
    core = lax.axis_index("core")
    sort_sides(lax.axis_index("yl") == 1, near_ref, far_ref, before_ref, after_ref)
    cot, before, after = (r[...].reshape(1024, C) for r in (cot_ref, before_ref, after_ref))
    zero = jnp.zeros((C, C), BF16)
    w_pair = jnp.concatenate(
        [
            jnp.concatenate([wd_ref[2], wd_ref[0]], axis=1),
            jnp.concatenate([zero, wd_ref[1]], axis=1),
        ],
        axis=0,
    )
    low = mm_nt(jnp.concatenate([before, cot], axis=1), w_pair).astype(BF16)
    high = mm_nt(jnp.concatenate([cot, after], axis=1), w_pair).astype(BF16)
    g_m1 = jnp.where(first, jnp.zeros_like(low[:, :C]), low[:, :C])
    g_0, g_1, g_2 = low[:, C:], high[:, :C], high[:, C:]
    w_time = jnp.concatenate(
        [
            jnp.concatenate([wt_ref[2], wt_ref[1], wt_ref[0], zero], axis=1),
            jnp.concatenate([zero, wt_ref[2], wt_ref[1], wt_ref[0]], axis=1),
        ],
        axis=0,
    )
    g_act = mm_nt(jnp.concatenate([g_m1, g_0, g_1, g_2], axis=1), w_time)
    spatial = None
    for f in range(2):
        gp = (g_act[:, f * C : (f + 1) * C] * slope_ref[f].reshape(1024, C)).astype(BF16)
        gpre_ref[f] = gp.reshape(8, 128, C)
        behind, here, ahead = columns(gp)
        shifted = jnp.concatenate([ahead, here, behind], axis=1)
        xt = jnp.concatenate([xt_ref[f, :, dy * 128 : dy * 128 + 1024] for dy in range(3)], axis=0)
        term = mm(xt, shifted)
        spatial = term if spatial is None else spatial + term
    row = 7 * (1 - core)
    for f in range(2):
        to_near_ref[f] = gpre_ref[f, row]
        to_far_ref[f] = gpre_ref[f, 7 - row]
    for dy in range(3):
        for dx in range(3):
            mats_ref[dy * 3 + dx] = spatial[dy * C : (dy + 1) * C, dx * C : (dx + 1) * C].reshape(2, 64, C)
    a0, a1 = at_ref[0], at_ref[1]
    x0, x1 = xt_ref[0, :, 128:1152], xt_ref[1, :, 128:1152]
    time = mm(a0, jnp.concatenate([g_1, g_0, g_m1], axis=1))
    time = time + mm(a1, jnp.concatenate([g_2, g_1, g_0], axis=1))
    for k in range(3):
        mats_ref[9 + k] = time[:, k * C : (k + 1) * C].reshape(2, 64, C)
    both = mm(
        jnp.concatenate([a0, a1, x0, x1], axis=0), jnp.concatenate([cot, after], axis=1)
    )
    tail = mm(a0, before)
    m_0, m_1 = both[0:128, :C], both[128:256, :C]
    m_m2, m_m1 = both[0:128, C:], both[128:256, C:]
    skip = jnp.where(first, jnp.zeros_like(m_0), m_0)
    kinds = (
        (both[384:512, C:], (m_m2, m_m1, skip)),
        (both[256:384, :C], (m_m1, m_0, m_1)),
        (both[384:512, :C], (m_0, m_1, tail)),
    )
    for k, (base, terms) in enumerate(kinds):
        total = base
        for tap, m in enumerate(terms):
            top = m.astype(BF16)
            rest = (m - top.astype(F32)).astype(BF16)
            total = total + mm_tn(wt_ref[tap], top) + mm_tn(wt_ref[tap], rest)
        mats_ref[12 + k] = total.reshape(2, 64, C)
    send_ref[...] = mats_ref[:, 1 - core].astype(BF16)
    keep_ref[...] = mats_ref[:, core]


def merge_kernel(keep_ref, got_ref, out_ref):
    out_ref[:15] = (keep_ref[...] + got_ref[...].astype(F32)).astype(BF16)
    out_ref[15] = jnp.zeros((64, C), BF16)


def down_kernel(x_ref, act_ref, near_ref, far_ref, wt_ref, wd_ref, out_ref, ahead_ref, after_ref):
    sort_sides(lax.axis_index("yl") == 1, near_ref, far_ref, ahead_ref, after_ref)
    zero = jnp.zeros((C, C), BF16)
    first = jnp.where(frame_index() == 0, zero, wt_ref[2])
    w_time = jnp.concatenate(
        [
            jnp.concatenate([first, wt_ref[1], wt_ref[0]], axis=1),
            jnp.concatenate([zero, wt_ref[2], wt_ref[1]], axis=1),
            jnp.concatenate([zero, zero, wt_ref[2]], axis=1),
        ],
        axis=0,
    )
    parts = [act_ref[0], act_ref[1], after_ref[...]]
    mixed = mm(jnp.concatenate([p.reshape(1024, C) for p in parts], axis=1), w_time)
    resid = [mixed[:, :C].astype(BF16)]
    for f in range(2):
        total = x_ref[f].astype(F32).reshape(1024, C) + mixed[:, (f + 1) * C : (f + 2) * C]
        resid.append(total.astype(BF16))
    weights = jnp.concatenate([wd_ref[0], wd_ref[1], wd_ref[2]], axis=0)
    down = mm(jnp.concatenate(resid, axis=1), weights)
    down = down + ahead_ref[...].reshape(1024, C).astype(F32)
    out_ref[...] = down.astype(BF16).reshape(8, 128, C)


def features_kernel(
    gpre_ref, g_near_ref, g_far_ref, cot_ref, near_ref, far_ref, w_ref, wd_ref,
    out_ref, wide_ref, rows_ref, before_ref, after_ref,
):
    wide_ref[...] = jnp.zeros_like(wide_ref)
    for out in range(2):
        for dy in range(3):
            for dx in range(3):
                start = ((dy + out) * 3 + dx) * C
                wide_ref[out * C : (out + 1) * C, start : start + C] = w_ref[2 - dy, 2 - dx]
    zero = jnp.zeros((C, C), BF16)
    w_pair = jnp.concatenate(
        [
            jnp.concatenate([wd_ref[1], zero], axis=1),
            jnp.concatenate([wd_ref[2], wd_ref[0]], axis=1),
        ],
        axis=0,
    )
    sort_sides(lax.axis_index("yl") == 1, near_ref, far_ref, before_ref, after_ref)
    sort_sides(lax.axis_index("core") == 1, g_near_ref, g_far_ref, rows_ref.at[:, 0], rows_ref.at[:, 9])
    rows_ref[:, 1:9] = gpre_ref[...]
    cot, after = (r[...].reshape(1024, C) for r in (cot_ref, after_ref))
    resid = mm_nt(jnp.concatenate([cot, after], axis=1), w_pair)
    for f in range(2):
        g = rows_ref[f].reshape(1280, C)
        conv = mm_nt(row_pairs(jnp.concatenate(columns(g), axis=1)), wide_ref[...])
        base = resid[:, f * C : (f + 1) * C].reshape(4, 2, 128, C)
        for out in range(2):
            part = conv[:, out * C : (out + 1) * C].reshape(4, 128, C)
            out_ref[f, :, out] = (base[:, out] + part).astype(BF16)


VMEM = pl.BlockSpec(memory_space=pltpu.VMEM)


def call(kernel, outs, args, taps, scratch=()):
    return pl.pallas_call(
        kernel,
        out_shape=[jax.ShapeDtypeStruct(s, d) for s, d in outs],
        in_specs=[VMEM] * len(args),
        out_specs=[VMEM] * len(outs),
        scratch_shapes=list(scratch),
        compiler_params=pltpu.CompilerParams(vmem_limit_bytes=24 * 1024 * 1024),
        cost_estimate=pl.CostEstimate(
            flops=int(taps * 2048 * C * C * 2), bytes_accessed=4_000_000, transcendentals=0
        ),
    )(*args)


def gather_kernel(mine_ref, other_ref, spatial_ref, time_ref, down_ref):
    mine = lax.axis_index("core") == 0
    low = jnp.where(mine, mine_ref[...], other_ref[...]).astype(F32)
    high = jnp.where(mine, other_ref[...], mine_ref[...]).astype(F32)
    for first, ref in ((0, spatial_ref), (9, time_ref), (12, down_ref)):
        count = ref.shape[0]
        ref[:, :64] = low[first : first + count]
        ref[:, 64:] = high[first : first + count]


def swap(x, axis, mask):
    return lax.ppermute(x, axis, [(i, i ^ mask) for i in range(lax.axis_size(axis))])


def swap_far(x, axis):
    count = lax.axis_size(axis)
    pairs = [(i, i + 1) for i in range(1, count - 1, 2)]
    return lax.ppermute(x, axis, pairs + [(b, a) for a, b in pairs])


def per_device(features, w_spatial, w_temporal, w_down, cotangent):
    time, rows = ("z", "yl"), ("x", "core")
    x, cot = features[0], cotangent[0, 0]
    frame, edge = ((8, 128, C), BF16), ((2, 128, C), BF16)
    frame_scratch, rows_scratch = pltpu.VMEM(*frame), pltpu.VMEM((2, 10, 128, C), BF16)
    cot_near, cot_far = swap(cot, time, 1), swap_far(cot, time)
    low, high = lax.optimization_barrier((x[:, 0], x[:, 7]))
    to_near, to_far = call(pick_kernel, [edge, edge], (low, high), 0)
    x_near, x_far = swap(to_near, rows, 1), swap_far(to_far, rows)
    slope, act, xt, at, to_near, to_far = call(
        forward_kernel,
        [((2, 4, 2, 128, C), F32), ((2, 4, 2, 128, C), BF16), ((2, C, 1280), BF16), ((2, C, 1024), BF16), frame, frame],
        (x, x_near, x_far, w_spatial, w_temporal, w_down), 11,
        scratch=[pltpu.VMEM((12 * C, 2 * C), BF16), rows_scratch],
    )
    t_near, t_far = swap(to_near, time, 1), swap_far(to_far, time)
    gpre, to_near, to_far, send, keep = call(
        grads_kernel,
        [((2, 8, 128, C), BF16), edge, edge, ((15, 64, C), BF16), ((15, 64, C), F32)],
        (slope, xt, at, cot, cot_near, cot_far, w_temporal, w_down), 21,
        scratch=[pltpu.VMEM((15, 2, 64, C), F32), frame_scratch, frame_scratch],
    )
    (half,) = call(merge_kernel, [((16, 64, C), BF16)], (keep, swap(send, "core", 1)), 0)
    got = lax.all_to_all(half, PLANE, 0, 0, tiled=True)
    got, to_near, to_far = lax.optimization_barrier((got, to_near, to_far))
    total = jnp.sum(got.astype(F32), axis=0)
    g_near, g_far = swap(to_near, rows, 1), swap_far(to_far, rows)
    total = total + swap(total, "z", 1)
    total = total + swap(total, "z", 2)
    total, t_near, t_far, g_near, g_far = lax.optimization_barrier((total, t_near, t_far, g_near, g_far))
    (down,) = call(
        down_kernel, [frame], (x, act.reshape(2, 8, 128, C), t_near, t_far, w_temporal, w_down), 5,
        scratch=[frame_scratch, frame_scratch],
    )
    total = total + swap(total, "z", 4)
    total, down = lax.optimization_barrier((total, down))
    out = jnp.broadcast_to(total.astype(BF16), (16, 64, C))
    out = lax.all_to_all(out, PLANE, 0, 0, tiled=True)
    (grad_features,) = call(
        features_kernel, [((2, 4, 2, 128, C), BF16)],
        (gpre, g_near, g_far, cot, cot_near, cot_far, w_spatial, w_down), 11,
        scratch=[pltpu.VMEM((2 * C, 12 * C), BF16), rows_scratch, frame_scratch, frame_scratch],
    )
    out, grad_features = lax.optimization_barrier((out, grad_features))
    grads = call(
        gather_kernel, [((n, C, C), F32) for n in (9, 3, 3)], (out, swap(out, "core", 1)), 0,
    )
    return (
        down[None, None],
        grad_features.reshape(1, 2, 8, 128, C),
        grads[0].reshape(3, 3, C, C),
        grads[1],
        grads[2],
    )


def solution(mesh):
    fine = Mesh(mesh.devices.reshape(2, 8, 2, 4, 2), ("yh", "z", "yl", "x", "core"))
    block = P("yh", ("z", "yl"), ("x", "core"), None, None)
    return jax.shard_map(
        per_device,
        mesh=fine,
        in_specs=(block, P(), P(), P(), block),
        out_specs=(block, block, P(), P(), P()),
        check_vma=False,
    )
```

```python
import jax
import jax.numpy as jnp
from jax import lax
from jax.experimental import pallas as pl
from jax.experimental.pallas import tpu as pltpu
from jax.sharding import Mesh, PartitionSpec as P

F32, BF16 = jnp.float32, jnp.bfloat16
C = 128
PLANE = ("yh", "yl", "x")


def mm(a, b):
    return lax.dot_general(a, b, (((1,), (0,)), ((), ())), preferred_element_type=F32)


def mm_nt(a, b):
    return lax.dot_general(a, b, (((1,), (1,)), ((), ())), preferred_element_type=F32)


def mm_tn(a, b):
    return lax.dot_general(a, b, (((0,), (0,)), ((), ())), preferred_element_type=F32)


def columns(x):
    wide = x.astype(F32)
    count = wide.shape[0]
    col = lax.broadcasted_iota(jnp.int32, wide.shape, 0) % 128
    before = jnp.where(col == 0, 0.0, pltpu.roll(wide, 1, 0)).astype(BF16)
    after = jnp.where(col == 127, 0.0, pltpu.roll(wide, count - 1, 0)).astype(BF16)
    return before, x, after


def row_pairs(cat):
    depth = cat.shape[1]
    rows = cat.reshape(5, 2, 128, depth)
    even, odd = rows[:, 0], rows[:, 1]
    parts = [even[0:4], odd[0:4], even[1:5], odd[1:5]]
    return jnp.concatenate([p.reshape(512, depth) for p in parts], axis=1)


def frame_index():
    return lax.axis_index("z") * 2 + lax.axis_index("yl")


def sort_sides(odd, near_ref, far_ref, before_ref, after_ref):
    @pl.when(odd)
    def _():
        before_ref[...] = near_ref[...]
        after_ref[...] = far_ref[...]

    @pl.when(jnp.logical_not(odd))
    def _():
        before_ref[...] = far_ref[...]
        after_ref[...] = near_ref[...]


def sort_rows(near_ref, far_ref, low_ref, high_ref):
    @pl.when(lax.axis_index("core") == 1)
    def _():
        low_ref[...] = near_ref[...].reshape(128, C)
        high_ref[...] = far_ref[...]

    @pl.when(lax.axis_index("core") == 0)
    def _():
        low_ref[...] = far_ref[...]
        high_ref[...] = near_ref[...].reshape(128, C)


def pick_kernel(low_ref, high_ref, near_ref, far_ref):
    sort_sides(lax.axis_index("core") == 1, low_ref, high_ref, near_ref, far_ref)


def prepare_kernel(x_hbm, w_hbm, x_ref, wide_ref, w_ref, sem):
    copies = [
        pltpu.make_async_copy(w_hbm, w_ref, sem.at[0]),
        pltpu.make_async_copy(x_hbm, x_ref, sem.at[1]),
    ]
    for copy in copies:
        copy.start()
    wide_ref[...] = jnp.zeros_like(wide_ref)
    copies[0].wait()
    for out in range(2):
        for dy in range(3):
            for dx in range(3):
                start = ((dy + out) * 3 + dx) * C
                wide_ref[start : start + C, out * C : (out + 1) * C] = w_ref[dy, dx]
    copies[1].wait()


def forward_kernel(
    x_ref, near_ref, far_ref, wide_ref, wt_ref, wd_ref,
    slope_ref, act_ref, xt_ref, at_ref, to_near_ref, to_far_ref, rows_ref,
):
    sort_sides(lax.axis_index("core") == 1, near_ref, far_ref, rows_ref.at[:, 0], rows_ref.at[:, 9])
    rows_ref[:, 1:9] = x_ref[...]
    for f in range(2):
        x = rows_ref[f].reshape(1280, C)
        xt_ref[f] = x.T
        pre = mm(row_pairs(jnp.concatenate(columns(x), axis=1)), wide_ref[...])
        sig = 1.0 / (1.0 + jnp.exp(-pre))
        act = (pre * sig).astype(BF16)
        slope = sig * (1.0 + pre * (1.0 - sig))
        for out in range(2):
            part = slice(out * C, (out + 1) * C)
            act_ref[f, :, out] = act[:, part].reshape(4, 128, C)
            slope_ref[f, :, out] = slope[:, part].reshape(4, 128, C)
        at_ref[f] = act_ref[f].reshape(1024, C).T
    zero = jnp.zeros((C, C), BF16)
    a0, a1 = act_ref[0].reshape(1024, C), act_ref[1].reshape(1024, C)
    w_time = jnp.concatenate(
        [
            jnp.concatenate([wt_ref[0], zero], axis=1),
            jnp.concatenate([wt_ref[1], wt_ref[0]], axis=1),
        ],
        axis=0,
    )
    mixed = mm(jnp.concatenate([a0, a1], axis=1), w_time)
    last = (x_ref[1].reshape(1024, C).astype(F32) + mixed[:, :C]).astype(BF16)
    both = jnp.concatenate([last, mixed[:, C:].astype(BF16)], axis=1)
    ahead = mm(both, jnp.concatenate([wd_ref[0], wd_ref[1]], axis=0)).astype(BF16)
    odd = lax.axis_index("yl") == 1

    @pl.when(odd)
    def _():
        to_near_ref[...] = a0.reshape(8, 128, C)
        to_far_ref[...] = ahead.reshape(8, 128, C)

    @pl.when(jnp.logical_not(odd))
    def _():
        to_near_ref[...] = ahead.reshape(8, 128, C)
        to_far_ref[...] = a0.reshape(8, 128, C)


def grads_kernel(
    slope_ref, xt_ref, at_ref, cot_ref, near_ref, far_ref, wt_ref, wd_ref,
    gpre_ref, to_far_ref, send_ref, keep_ref, mats_ref, before_ref, after_ref,
):
    first = frame_index() == 0
    core = lax.axis_index("core")
    sort_sides(lax.axis_index("yl") == 1, near_ref, far_ref, before_ref, after_ref)
    cot, before, after = (r[...].reshape(1024, C) for r in (cot_ref, before_ref, after_ref))
    zero = jnp.zeros((C, C), BF16)
    w_pair = jnp.concatenate(
        [
            jnp.concatenate([wd_ref[2], wd_ref[0]], axis=1),
            jnp.concatenate([zero, wd_ref[1]], axis=1),
        ],
        axis=0,
    )
    low = mm_nt(jnp.concatenate([before, cot], axis=1), w_pair).astype(BF16)
    high = mm_nt(jnp.concatenate([cot, after], axis=1), w_pair).astype(BF16)
    g_m1 = jnp.where(first, jnp.zeros_like(low[:, :C]), low[:, :C])
    g_0, g_1, g_2 = low[:, C:], high[:, :C], high[:, C:]
    w_time = jnp.concatenate(
        [
            jnp.concatenate([wt_ref[2], wt_ref[1], wt_ref[0], zero], axis=1),
            jnp.concatenate([zero, wt_ref[2], wt_ref[1], wt_ref[0]], axis=1),
        ],
        axis=0,
    )
    g_act = mm_nt(jnp.concatenate([g_m1, g_0, g_1, g_2], axis=1), w_time)
    spatial = None
    for f in range(2):
        gp = (g_act[:, f * C : (f + 1) * C] * slope_ref[f].reshape(1024, C)).astype(BF16)
        gpre_ref[f] = gp.reshape(8, 128, C)
        behind, here, ahead = columns(gp)
        shifted = jnp.concatenate([ahead, here, behind], axis=1)
        xt = jnp.concatenate([xt_ref[f, :, dy * 128 : dy * 128 + 1024] for dy in range(3)], axis=0)
        term = mm(xt, shifted)
        spatial = term if spatial is None else spatial + term
    row = 7 * (1 - core)
    for f in range(2):
        send_ref[15 + 2 * f : 17 + 2 * f] = gpre_ref[f, row].reshape(2, 64, C)
        to_far_ref[f] = gpre_ref[f, 7 - row]
    for dy in range(3):
        for dx in range(3):
            mats_ref[dy * 3 + dx] = spatial[dy * C : (dy + 1) * C, dx * C : (dx + 1) * C].reshape(2, 64, C)
    a0, a1 = at_ref[0], at_ref[1]
    x0, x1 = xt_ref[0, :, 128:1152], xt_ref[1, :, 128:1152]
    time = mm(a0, jnp.concatenate([g_1, g_0, g_m1], axis=1))
    time = time + mm(a1, jnp.concatenate([g_2, g_1, g_0], axis=1))
    for k in range(3):
        mats_ref[9 + k] = time[:, k * C : (k + 1) * C].reshape(2, 64, C)
    both = mm(
        jnp.concatenate([a0, a1, x0, x1], axis=0), jnp.concatenate([cot, after], axis=1)
    )
    tail = mm(a0, before)
    m_0, m_1 = both[0:128, :C], both[128:256, :C]
    m_m2, m_m1 = both[0:128, C:], both[128:256, C:]
    skip = jnp.where(first, jnp.zeros_like(m_0), m_0)
    kinds = (
        (both[384:512, C:], (m_m2, m_m1, skip)),
        (both[256:384, :C], (m_m1, m_0, m_1)),
        (both[384:512, :C], (m_0, m_1, tail)),
    )
    for k, (base, terms) in enumerate(kinds):
        total = base
        for tap, m in enumerate(terms):
            top = m.astype(BF16)
            rest = (m - top.astype(F32)).astype(BF16)
            total = total + mm_tn(wt_ref[tap], top) + mm_tn(wt_ref[tap], rest)
        mats_ref[12 + k] = total.reshape(2, 64, C)
    send_ref[:15] = mats_ref[:, 1 - core].astype(BF16)
    keep_ref[...] = mats_ref[:, core]


def merge_kernel(keep_ref, got_ref, out_ref):
    out_ref[:15] = (keep_ref[...] + got_ref[:15].astype(F32)).astype(BF16)
    out_ref[15] = jnp.zeros((64, C), BF16)


def down_kernel(x_ref, act_ref, near_ref, far_ref, wt_ref, wd_ref, out_ref, ahead_ref, after_ref):
    sort_sides(lax.axis_index("yl") == 1, near_ref, far_ref, ahead_ref, after_ref)
    zero = jnp.zeros((C, C), BF16)
    first = jnp.where(frame_index() == 0, zero, wt_ref[2])
    w_time = jnp.concatenate(
        [
            jnp.concatenate([first, wt_ref[1], wt_ref[0]], axis=1),
            jnp.concatenate([zero, wt_ref[2], wt_ref[1]], axis=1),
            jnp.concatenate([zero, zero, wt_ref[2]], axis=1),
        ],
        axis=0,
    )
    parts = [act_ref[0], act_ref[1], after_ref[...]]
    mixed = mm(jnp.concatenate([p.reshape(1024, C) for p in parts], axis=1), w_time)
    resid = [mixed[:, :C].astype(BF16)]
    for f in range(2):
        total = x_ref[f].astype(F32).reshape(1024, C) + mixed[:, (f + 1) * C : (f + 2) * C]
        resid.append(total.astype(BF16))
    weights = jnp.concatenate([wd_ref[0], wd_ref[1], wd_ref[2]], axis=0)
    down = mm(jnp.concatenate(resid, axis=1), weights)
    down = down + ahead_ref[...].reshape(1024, C).astype(F32)
    out_ref[...] = down.astype(BF16).reshape(8, 128, C)


def features_kernel(
    gpre_ref, sent_ref, g_far_ref, cot_ref, near_ref, far_ref, w_ref, wd_ref,
    out_ref, wide_ref, rows_ref, before_ref, after_ref,
):
    wide_ref[...] = jnp.zeros_like(wide_ref)
    for out in range(2):
        for dy in range(3):
            for dx in range(3):
                start = ((dy + out) * 3 + dx) * C
                wide_ref[out * C : (out + 1) * C, start : start + C] = w_ref[2 - dy, 2 - dx]
    zero = jnp.zeros((C, C), BF16)
    w_pair = jnp.concatenate(
        [
            jnp.concatenate([wd_ref[1], zero], axis=1),
            jnp.concatenate([wd_ref[2], wd_ref[0]], axis=1),
        ],
        axis=0,
    )
    sort_sides(lax.axis_index("yl") == 1, near_ref, far_ref, before_ref, after_ref)
    for f in range(2):
        near_ref_f = sent_ref.at[15 + 2 * f : 17 + 2 * f]
        sort_rows(near_ref_f, g_far_ref.at[f], rows_ref.at[f, 0], rows_ref.at[f, 9])
    rows_ref[:, 1:9] = gpre_ref[...]
    cot, after = (r[...].reshape(1024, C) for r in (cot_ref, after_ref))
    resid = mm_nt(jnp.concatenate([cot, after], axis=1), w_pair)
    for f in range(2):
        g = rows_ref[f].reshape(1280, C)
        conv = mm_nt(row_pairs(jnp.concatenate(columns(g), axis=1)), wide_ref[...])
        base = resid[:, f * C : (f + 1) * C].reshape(4, 2, 128, C)
        for out in range(2):
            part = conv[:, out * C : (out + 1) * C].reshape(4, 128, C)
            out_ref[f, :, out] = (base[:, out] + part).astype(BF16)


VMEM = pl.BlockSpec(memory_space=pltpu.VMEM)


def call(kernel, outs, args, taps, scratch=()):
    return pl.pallas_call(
        kernel,
        out_shape=[jax.ShapeDtypeStruct(s, d) for s, d in outs],
        in_specs=[VMEM] * len(args),
        out_specs=[VMEM] * len(outs),
        scratch_shapes=list(scratch),
        compiler_params=pltpu.CompilerParams(vmem_limit_bytes=24 * 1024 * 1024),
        cost_estimate=pl.CostEstimate(
            flops=int(taps * 2048 * C * C * 2), bytes_accessed=4_000_000, transcendentals=0
        ),
    )(*args)


def gather_kernel(mine_ref, other_ref, spatial_ref, time_ref, down_ref):
    mine = lax.axis_index("core") == 0
    low = jnp.where(mine, mine_ref[...], other_ref[...]).astype(F32)
    high = jnp.where(mine, other_ref[...], mine_ref[...]).astype(F32)
    for first, ref in ((0, spatial_ref), (9, time_ref), (12, down_ref)):
        count = ref.shape[0]
        ref[:, :64] = low[first : first + count]
        ref[:, 64:] = high[first : first + count]


def exchange(x, axis, count):
    groups = [list(range(count - 1, -1, -1))]
    return lax.all_to_all(x, axis, 0, 0, axis_index_groups=groups, tiled=True)


def swap(x, axis, mask):
    return lax.ppermute(x, axis, [(i, i ^ mask) for i in range(lax.axis_size(axis))])


def swap_far(x, axis):
    count = lax.axis_size(axis)
    pairs = [(i, i + 1) for i in range(1, count - 1, 2)]
    return lax.ppermute(x, axis, pairs + [(b, a) for a, b in pairs])


def per_device(features, w_spatial, w_temporal, w_down, cotangent):
    time, rows = ("z", "yl"), ("x", "core")
    x, cot = features[0], cotangent[0, 0]
    frame, edge = ((8, 128, C), BF16), ((2, 128, C), BF16)
    frame_scratch, rows_scratch = pltpu.VMEM(*frame), pltpu.VMEM((2, 10, 128, C), BF16)
    cot_near, cot_far = swap(cot, time, 1), swap_far(cot, time)
    low, high = lax.optimization_barrier((x[:, 0], x[:, 7]))
    to_near, to_far = call(pick_kernel, [edge, edge], (low, high), 0)
    x_near, x_far = swap(to_near, rows, 1), swap_far(to_far, rows)
    source, _ = lax.optimization_barrier((x, to_near))
    here, wide = pl.pallas_call(
        prepare_kernel,
        out_shape=[jax.ShapeDtypeStruct((2, 8, 128, C), BF16), jax.ShapeDtypeStruct((12 * C, 2 * C), BF16)],
        in_specs=[pl.BlockSpec(memory_space=pl.ANY)] * 2,
        out_specs=[VMEM] * 2,
        scratch_shapes=[pltpu.VMEM((3, 3, C, C), BF16), pltpu.SemaphoreType.DMA((2,))],
        compiler_params=pltpu.CompilerParams(vmem_limit_bytes=24 * 1024 * 1024),
    )(source, w_spatial)
    slope, act, xt, at, to_near, to_far = call(
        forward_kernel,
        [((2, 4, 2, 128, C), F32), ((2, 4, 2, 128, C), BF16), ((2, C, 1280), BF16), ((2, C, 1024), BF16), frame, frame],
        (here, x_near, x_far, wide, w_temporal, w_down), 11,
        scratch=[rows_scratch],
    )
    t_near, t_far = swap(to_near, time, 1), swap_far(to_far, time)
    gpre, to_far, send, keep = call(
        grads_kernel,
        [((2, 8, 128, C), BF16), edge, ((19, 64, C), BF16), ((15, 64, C), F32)],
        (slope, xt, at, cot, cot_near, cot_far, w_temporal, w_down), 21,
        scratch=[pltpu.VMEM((15, 2, 64, C), F32), frame_scratch, frame_scratch],
    )
    near = swap(send, "core", 1)
    (half,) = call(merge_kernel, [((16, 64, C), BF16)], (keep, near), 0)
    got = exchange(half, PLANE, 16)
    got, to_far = lax.optimization_barrier((got, to_far))
    total = jnp.sum(got.astype(F32), axis=0)
    g_far = swap_far(to_far, rows)
    column = jnp.broadcast_to(total.astype(BF16), (8, 64, C))
    column = exchange(column, "z", 8)
    column, g_far, t_near, t_far = lax.optimization_barrier((column, g_far, t_near, t_far))
    total = jnp.sum(column.astype(F32), axis=0)
    out = jnp.broadcast_to(total.astype(BF16), (16, 64, C))
    out = exchange(out, PLANE, 16)
    (down,) = call(
        down_kernel, [frame], (x, act.reshape(2, 8, 128, C), t_near, t_far, w_temporal, w_down), 5,
        scratch=[frame_scratch, frame_scratch],
    )
    (grad_features,) = call(
        features_kernel, [((2, 4, 2, 128, C), BF16)],
        (gpre, near, g_far, cot, cot_near, cot_far, w_spatial, w_down), 11,
        scratch=[pltpu.VMEM((2 * C, 12 * C), BF16), rows_scratch, frame_scratch, frame_scratch],
    )
    out, down, grad_features = lax.optimization_barrier((out, down, grad_features))
    grads = call(
        gather_kernel, [((n, C, C), F32) for n in (9, 3, 3)], (out, swap(out, "core", 1)), 0,
    )
    return (
        down[None, None],
        grad_features.reshape(1, 2, 8, 128, C),
        grads[0].reshape(3, 3, C, C),
        grads[1],
        grads[2],
    )


def solution(mesh):
    fine = Mesh(mesh.devices.reshape(2, 8, 2, 4, 2), ("yh", "z", "yl", "x", "core"))
    block = P("yh", ("z", "yl"), ("x", "core"), None, None)
    return jax.shard_map(
        per_device,
        mesh=fine,
        in_specs=(block, P(), P(), P(), block),
        out_specs=(block, block, P(), P(), P()),
        check_vma=False,
    )
```

```python
import jax
import jax.numpy as jnp
from jax import lax
from jax.experimental import pallas as pl
from jax.experimental.pallas import tpu as pltpu
from jax.sharding import Mesh, PartitionSpec as P

F32, BF16 = jnp.float32, jnp.bfloat16
C = 128
PLANE = ("yh", "yl", "x")


def mm(a, b):
    return lax.dot_general(a, b, (((1,), (0,)), ((), ())), preferred_element_type=F32)


def mm_nt(a, b):
    return lax.dot_general(a, b, (((1,), (1,)), ((), ())), preferred_element_type=F32)


def mm_tn(a, b):
    return lax.dot_general(a, b, (((0,), (0,)), ((), ())), preferred_element_type=F32)


def columns(x):
    wide = x.astype(F32)
    count = wide.shape[0]
    col = lax.broadcasted_iota(jnp.int32, wide.shape, 0) % 128
    before = jnp.where(col == 0, 0.0, pltpu.roll(wide, 1, 0)).astype(BF16)
    after = jnp.where(col == 127, 0.0, pltpu.roll(wide, count - 1, 0)).astype(BF16)
    return before, x, after


def row_pairs(cat):
    depth = cat.shape[1]
    rows = cat.reshape(5, 2, 128, depth)
    even, odd = rows[:, 0], rows[:, 1]
    parts = [even[0:4], odd[0:4], even[1:5], odd[1:5]]
    return jnp.concatenate([p.reshape(512, depth) for p in parts], axis=1)


def frame_index():
    return lax.axis_index("z") * 2 + lax.axis_index("yl")


def sort_sides(odd, near_ref, far_ref, before_ref, after_ref):
    @pl.when(odd)
    def _():
        before_ref[...] = near_ref[...]
        after_ref[...] = far_ref[...]

    @pl.when(jnp.logical_not(odd))
    def _():
        before_ref[...] = far_ref[...]
        after_ref[...] = near_ref[...]


def sort_rows(near_ref, far_ref, low_ref, high_ref):
    @pl.when(lax.axis_index("core") == 1)
    def _():
        low_ref[...] = near_ref[...].reshape(128, C)
        high_ref[...] = far_ref[...]

    @pl.when(lax.axis_index("core") == 0)
    def _():
        low_ref[...] = far_ref[...]
        high_ref[...] = near_ref[...].reshape(128, C)


def pick_kernel(low_ref, high_ref, near_ref, far_ref):
    sort_sides(lax.axis_index("core") == 1, low_ref, high_ref, near_ref, far_ref)


def prepare_kernel(x_hbm, w_hbm, x_ref, wide_ref, w_ref, sem):
    copies = [
        pltpu.make_async_copy(w_hbm, w_ref, sem.at[0]),
        pltpu.make_async_copy(x_hbm, x_ref, sem.at[1]),
    ]
    for copy in copies:
        copy.start()
    wide_ref[...] = jnp.zeros_like(wide_ref)
    copies[0].wait()
    for out in range(2):
        for dy in range(3):
            for dx in range(3):
                start = ((dy + out) * 3 + dx) * C
                wide_ref[start : start + C, out * C : (out + 1) * C] = w_ref[dy, dx]
    copies[1].wait()


def forward_kernel(
    x_ref, near_ref, far_ref, wide_ref, wt_ref, wd_ref,
    slope_ref, act_ref, xt_ref, at_ref, to_near_ref, to_far_ref, rows_ref,
):
    sort_sides(lax.axis_index("core") == 1, near_ref, far_ref, rows_ref.at[:, 0], rows_ref.at[:, 9])
    rows_ref[:, 1:9] = x_ref[...]
    for f in range(2):
        x = rows_ref[f].reshape(1280, C)
        xt_ref[f] = x.T
        pre = mm(row_pairs(jnp.concatenate(columns(x), axis=1)), wide_ref[...])
        sig = 1.0 / (1.0 + jnp.exp(-pre))
        act = (pre * sig).astype(BF16)
        slope = sig * (1.0 + pre * (1.0 - sig))
        for out in range(2):
            part = slice(out * C, (out + 1) * C)
            act_ref[f, :, out] = act[:, part].reshape(4, 128, C)
            slope_ref[f, :, out] = slope[:, part].reshape(4, 128, C)
        at_ref[f] = act_ref[f].reshape(1024, C).T
    zero = jnp.zeros((C, C), BF16)
    a0, a1 = act_ref[0].reshape(1024, C), act_ref[1].reshape(1024, C)
    w_time = jnp.concatenate(
        [
            jnp.concatenate([wt_ref[0], zero], axis=1),
            jnp.concatenate([wt_ref[1], wt_ref[0]], axis=1),
        ],
        axis=0,
    )
    mixed = mm(jnp.concatenate([a0, a1], axis=1), w_time)
    last = (x_ref[1].reshape(1024, C).astype(F32) + mixed[:, :C]).astype(BF16)
    both = jnp.concatenate([last, mixed[:, C:].astype(BF16)], axis=1)
    ahead = mm(both, jnp.concatenate([wd_ref[0], wd_ref[1]], axis=0)).astype(BF16)
    odd = lax.axis_index("yl") == 1

    @pl.when(odd)
    def _():
        to_near_ref[...] = a0.reshape(8, 128, C)
        to_far_ref[...] = ahead.reshape(8, 128, C)

    @pl.when(jnp.logical_not(odd))
    def _():
        to_near_ref[...] = ahead.reshape(8, 128, C)
        to_far_ref[...] = a0.reshape(8, 128, C)


def grads_kernel(
    slope_ref, xt_ref, at_ref, cot_ref, near_ref, far_ref, wt_ref, wd_ref,
    gpre_ref, to_far_ref, send_ref, keep_ref, mats_ref, before_ref, after_ref,
):
    first = frame_index() == 0
    core = lax.axis_index("core")
    sort_sides(lax.axis_index("yl") == 1, near_ref, far_ref, before_ref, after_ref)
    cot, before, after = (r[...].reshape(1024, C) for r in (cot_ref, before_ref, after_ref))
    zero = jnp.zeros((C, C), BF16)
    w_pair = jnp.concatenate(
        [
            jnp.concatenate([wd_ref[2], wd_ref[0]], axis=1),
            jnp.concatenate([zero, wd_ref[1]], axis=1),
        ],
        axis=0,
    )
    low = mm_nt(jnp.concatenate([before, cot], axis=1), w_pair).astype(BF16)
    high = mm_nt(jnp.concatenate([cot, after], axis=1), w_pair).astype(BF16)
    g_m1 = jnp.where(first, jnp.zeros_like(low[:, :C]), low[:, :C])
    g_0, g_1, g_2 = low[:, C:], high[:, :C], high[:, C:]
    w_time = jnp.concatenate(
        [
            jnp.concatenate([wt_ref[2], wt_ref[1], wt_ref[0], zero], axis=1),
            jnp.concatenate([zero, wt_ref[2], wt_ref[1], wt_ref[0]], axis=1),
        ],
        axis=0,
    )
    g_act = mm_nt(jnp.concatenate([g_m1, g_0, g_1, g_2], axis=1), w_time)
    spatial = None
    for f in range(2):
        gp = (g_act[:, f * C : (f + 1) * C] * slope_ref[f].reshape(1024, C)).astype(BF16)
        gpre_ref[f] = gp.reshape(8, 128, C)
        behind, here, ahead = columns(gp)
        shifted = jnp.concatenate([ahead, here, behind], axis=1)
        xt = jnp.concatenate([xt_ref[f, :, dy * 128 : dy * 128 + 1024] for dy in range(3)], axis=0)
        term = mm(xt, shifted)
        spatial = term if spatial is None else spatial + term
    row = 7 * (1 - core)
    for f in range(2):
        send_ref[15 + 2 * f : 17 + 2 * f] = gpre_ref[f, row].reshape(2, 64, C)
        to_far_ref[f] = gpre_ref[f, 7 - row]
    for dy in range(3):
        for dx in range(3):
            mats_ref[dy * 3 + dx] = spatial[dy * C : (dy + 1) * C, dx * C : (dx + 1) * C].reshape(2, 64, C)
    a0, a1 = at_ref[0], at_ref[1]
    x0, x1 = xt_ref[0, :, 128:1152], xt_ref[1, :, 128:1152]
    time = mm(a0, jnp.concatenate([g_1, g_0, g_m1], axis=1))
    time = time + mm(a1, jnp.concatenate([g_2, g_1, g_0], axis=1))
    for k in range(3):
        mats_ref[9 + k] = time[:, k * C : (k + 1) * C].reshape(2, 64, C)
    both = mm(
        jnp.concatenate([a0, a1, x0, x1], axis=0), jnp.concatenate([cot, after], axis=1)
    )
    tail = mm(a0, before)
    m_0, m_1 = both[0:128, :C], both[128:256, :C]
    m_m2, m_m1 = both[0:128, C:], both[128:256, C:]
    skip = jnp.where(first, jnp.zeros_like(m_0), m_0)
    kinds = (
        (both[384:512, C:], (m_m2, m_m1, skip)),
        (both[256:384, :C], (m_m1, m_0, m_1)),
        (both[384:512, :C], (m_0, m_1, tail)),
    )
    for k, (base, terms) in enumerate(kinds):
        total = base
        for tap, m in enumerate(terms):
            top = m.astype(BF16)
            rest = (m - top.astype(F32)).astype(BF16)
            total = total + mm_tn(wt_ref[tap], top) + mm_tn(wt_ref[tap], rest)
        mats_ref[12 + k] = total.reshape(2, 64, C)
    send_ref[:15] = mats_ref[:, 1 - core].astype(BF16)
    keep_ref[...] = mats_ref[:, core]


def merge_kernel(keep_ref, got_ref, out_ref):
    out_ref[:15] = (keep_ref[...] + got_ref[:15].astype(F32)).astype(BF16)
    out_ref[15] = jnp.zeros((64, C), BF16)


def down_kernel(x_ref, act_ref, near_ref, far_ref, wt_ref, wd_ref, out_ref, ahead_ref, after_ref):
    sort_sides(lax.axis_index("yl") == 1, near_ref, far_ref, ahead_ref, after_ref)
    zero = jnp.zeros((C, C), BF16)
    first = jnp.where(frame_index() == 0, zero, wt_ref[2])
    w_time = jnp.concatenate(
        [
            jnp.concatenate([first, wt_ref[1], wt_ref[0]], axis=1),
            jnp.concatenate([zero, wt_ref[2], wt_ref[1]], axis=1),
            jnp.concatenate([zero, zero, wt_ref[2]], axis=1),
        ],
        axis=0,
    )
    parts = [act_ref[0], act_ref[1], after_ref[...]]
    mixed = mm(jnp.concatenate([p.reshape(1024, C) for p in parts], axis=1), w_time)
    resid = [mixed[:, :C].astype(BF16)]
    for f in range(2):
        total = x_ref[f].astype(F32).reshape(1024, C) + mixed[:, (f + 1) * C : (f + 2) * C]
        resid.append(total.astype(BF16))
    weights = jnp.concatenate([wd_ref[0], wd_ref[1], wd_ref[2]], axis=0)
    down = mm(jnp.concatenate(resid, axis=1), weights)
    down = down + ahead_ref[...].reshape(1024, C).astype(F32)
    out_ref[...] = down.astype(BF16).reshape(8, 128, C)


def features_kernel(
    gpre_ref, sent_ref, g_far_ref, cot_ref, near_ref, far_ref, w_ref, wd_ref,
    out_ref, wide_ref, rows_ref, before_ref, after_ref,
):
    wide_ref[...] = jnp.zeros_like(wide_ref)
    for out in range(2):
        for dy in range(3):
            for dx in range(3):
                start = ((dy + out) * 3 + dx) * C
                wide_ref[out * C : (out + 1) * C, start : start + C] = w_ref[2 - dy, 2 - dx]
    zero = jnp.zeros((C, C), BF16)
    w_pair = jnp.concatenate(
        [
            jnp.concatenate([wd_ref[1], zero], axis=1),
            jnp.concatenate([wd_ref[2], wd_ref[0]], axis=1),
        ],
        axis=0,
    )
    sort_sides(lax.axis_index("yl") == 1, near_ref, far_ref, before_ref, after_ref)
    for f in range(2):
        near_ref_f = sent_ref.at[15 + 2 * f : 17 + 2 * f]
        sort_rows(near_ref_f, g_far_ref.at[f], rows_ref.at[f, 0], rows_ref.at[f, 9])
    rows_ref[:, 1:9] = gpre_ref[...]
    cot, after = (r[...].reshape(1024, C) for r in (cot_ref, after_ref))
    resid = mm_nt(jnp.concatenate([cot, after], axis=1), w_pair)
    for f in range(2):
        g = rows_ref[f].reshape(1280, C)
        conv = mm_nt(row_pairs(jnp.concatenate(columns(g), axis=1)), wide_ref[...])
        base = resid[:, f * C : (f + 1) * C].reshape(4, 2, 128, C)
        for out in range(2):
            part = conv[:, out * C : (out + 1) * C].reshape(4, 128, C)
            out_ref[f, :, out] = (base[:, out] + part).astype(BF16)


VMEM = pl.BlockSpec(memory_space=pltpu.VMEM)


def call(kernel, outs, args, taps, scratch=()):
    return pl.pallas_call(
        kernel,
        out_shape=[jax.ShapeDtypeStruct(s, d) for s, d in outs],
        in_specs=[VMEM] * len(args),
        out_specs=[VMEM] * len(outs),
        scratch_shapes=list(scratch),
        compiler_params=pltpu.CompilerParams(vmem_limit_bytes=24 * 1024 * 1024),
        cost_estimate=pl.CostEstimate(
            flops=int(taps * 2048 * C * C * 2), bytes_accessed=4_000_000, transcendentals=0
        ),
    )(*args)


def gather_kernel(mine_ref, other_ref, spatial_ref, time_ref, down_ref):
    mine = lax.axis_index("core") == 0
    low = jnp.where(mine, mine_ref[...], other_ref[...]).astype(F32)
    high = jnp.where(mine, other_ref[...], mine_ref[...]).astype(F32)
    for first, ref in ((0, spatial_ref), (9, time_ref), (12, down_ref)):
        count = ref.shape[0]
        ref[:, :64] = low[first : first + count]
        ref[:, 64:] = high[first : first + count]


def exchange(x, axis, count):
    groups = [list(range(count - 1, -1, -1))]
    return lax.all_to_all(x, axis, 0, 0, axis_index_groups=groups, tiled=True)


def swap(x, axis, mask):
    return lax.ppermute(x, axis, [(i, i ^ mask) for i in range(lax.axis_size(axis))])


def swap_far(x, axis):
    count = lax.axis_size(axis)
    pairs = [(i, i + 1) for i in range(1, count - 1, 2)]
    return lax.ppermute(x, axis, pairs + [(b, a) for a, b in pairs])


def per_device(features, w_spatial, w_temporal, w_down, cotangent):
    time, rows = ("z", "yl"), ("x", "core")
    x, cot = features[0], cotangent[0, 0]
    frame, edge = ((8, 128, C), BF16), ((2, 128, C), BF16)
    frame_scratch, rows_scratch = pltpu.VMEM(*frame), pltpu.VMEM((2, 10, 128, C), BF16)
    cot_near, cot_far = swap(cot, time, 1), swap_far(cot, time)
    low, high = lax.optimization_barrier((x[:, 0], x[:, 7]))
    to_near, to_far = call(pick_kernel, [edge, edge], (low, high), 0)
    x_near, x_far = swap(to_near, rows, 1), swap_far(to_far, rows)
    source, _ = lax.optimization_barrier((x, to_near))
    here, wide = pl.pallas_call(
        prepare_kernel,
        out_shape=[jax.ShapeDtypeStruct((2, 8, 128, C), BF16), jax.ShapeDtypeStruct((12 * C, 2 * C), BF16)],
        in_specs=[pl.BlockSpec(memory_space=pl.ANY)] * 2,
        out_specs=[VMEM] * 2,
        scratch_shapes=[pltpu.VMEM((3, 3, C, C), BF16), pltpu.SemaphoreType.DMA((2,))],
        compiler_params=pltpu.CompilerParams(vmem_limit_bytes=24 * 1024 * 1024),
    )(source, w_spatial)
    slope, act, xt, at, to_near, to_far = call(
        forward_kernel,
        [((2, 4, 2, 128, C), F32), ((2, 4, 2, 128, C), BF16), ((2, C, 1280), BF16), ((2, C, 1024), BF16), frame, frame],
        (here, x_near, x_far, wide, w_temporal, w_down), 11,
        scratch=[rows_scratch],
    )
    to_t_near, to_t_far = to_near, to_far
    gpre, to_far, send, keep = call(
        grads_kernel,
        [((2, 8, 128, C), BF16), edge, ((19, 64, C), BF16), ((15, 64, C), F32)],
        (slope, xt, at, cot, cot_near, cot_far, w_temporal, w_down), 21,
        scratch=[pltpu.VMEM((15, 2, 64, C), F32), frame_scratch, frame_scratch],
    )
    near = swap(send, "core", 1)
    (half,) = call(merge_kernel, [((16, 64, C), BF16)], (keep, near), 0)
    got = exchange(half, PLANE, 16)
    got, to_far, to_t_near, to_t_far = lax.optimization_barrier((got, to_far, to_t_near, to_t_far))
    total = jnp.sum(got.astype(F32), axis=0)
    t_near, t_far = swap(to_t_near, time, 1), swap_far(to_t_far, time)
    g_far = swap_far(to_far, rows)
    column = jnp.broadcast_to(total.astype(BF16), (8, 64, C))
    column = exchange(column, "z", 8)
    column, g_far = lax.optimization_barrier((column, g_far))
    total = jnp.sum(column.astype(F32), axis=0)
    out = jnp.broadcast_to(total.astype(BF16), (16, 64, C))
    out = exchange(out, PLANE, 16)
    (down,) = call(
        down_kernel, [frame], (x, act.reshape(2, 8, 128, C), t_near, t_far, w_temporal, w_down), 5,
        scratch=[frame_scratch, frame_scratch],
    )
    (grad_features,) = call(
        features_kernel, [((2, 4, 2, 128, C), BF16)],
        (gpre, near, g_far, cot, cot_near, cot_far, w_spatial, w_down), 11,
        scratch=[pltpu.VMEM((2 * C, 12 * C), BF16), rows_scratch, frame_scratch, frame_scratch],
    )
    out, down, grad_features = lax.optimization_barrier((out, down, grad_features))
    grads = call(
        gather_kernel, [((n, C, C), F32) for n in (9, 3, 3)], (out, swap(out, "core", 1)), 0,
    )
    return (
        down[None, None],
        grad_features.reshape(1, 2, 8, 128, C),
        grads[0].reshape(3, 3, C, C),
        grads[1],
        grads[2],
    )


def solution(mesh):
    fine = Mesh(mesh.devices.reshape(2, 8, 2, 4, 2), ("yh", "z", "yl", "x", "core"))
    block = P("yh", ("z", "yl"), ("x", "core"), None, None)
    return jax.shard_map(
        per_device,
        mesh=fine,
        in_specs=(block, P(), P(), P(), block),
        out_specs=(block, block, P(), P(), P()),
        check_vma=False,
    )
```

```python
import jax
import jax.numpy as jnp
from jax import lax
from jax.experimental import pallas as pl
from jax.experimental.pallas import tpu as pltpu
from jax.sharding import Mesh, PartitionSpec as P

F32, BF16 = jnp.float32, jnp.bfloat16
C = 128
PLANE = ("yh", "yl", "x")


def mm(a, b):
    return lax.dot_general(a, b, (((1,), (0,)), ((), ())), preferred_element_type=F32)


def mm_nt(a, b):
    return lax.dot_general(a, b, (((1,), (1,)), ((), ())), preferred_element_type=F32)


def mm_tn(a, b):
    return lax.dot_general(a, b, (((0,), (0,)), ((), ())), preferred_element_type=F32)


def columns(x):
    wide = x.astype(F32)
    count = wide.shape[0]
    col = lax.broadcasted_iota(jnp.int32, wide.shape, 0) % 128
    before = jnp.where(col == 0, 0.0, pltpu.roll(wide, 1, 0)).astype(BF16)
    after = jnp.where(col == 127, 0.0, pltpu.roll(wide, count - 1, 0)).astype(BF16)
    return before, x, after


def row_pairs(cat):
    depth = cat.shape[1]
    rows = cat.reshape(5, 2, 128, depth)
    even, odd = rows[:, 0], rows[:, 1]
    parts = [even[0:4], odd[0:4], even[1:5], odd[1:5]]
    return jnp.concatenate([p.reshape(512, depth) for p in parts], axis=1)


def frame_index():
    return lax.axis_index("z") * 2 + lax.axis_index("yl")


def sort_sides(odd, near_ref, far_ref, before_ref, after_ref):
    @pl.when(odd)
    def _():
        before_ref[...] = near_ref[...]
        after_ref[...] = far_ref[...]

    @pl.when(jnp.logical_not(odd))
    def _():
        before_ref[...] = far_ref[...]
        after_ref[...] = near_ref[...]


def sort_rows(near_ref, far_ref, low_ref, high_ref):
    @pl.when(lax.axis_index("core") == 1)
    def _():
        low_ref[...] = near_ref[...].reshape(128, C)
        high_ref[...] = far_ref[...]

    @pl.when(lax.axis_index("core") == 0)
    def _():
        low_ref[...] = far_ref[...]
        high_ref[...] = near_ref[...].reshape(128, C)


def pick_kernel(low_ref, high_ref, near_ref, far_ref):
    sort_sides(lax.axis_index("core") == 1, low_ref, high_ref, near_ref, far_ref)


def prepare_kernel(x_hbm, w_hbm, x_ref, wide_ref, turn_ref, w_ref, sem):
    copies = [
        pltpu.make_async_copy(w_hbm, w_ref, sem.at[0]),
        pltpu.make_async_copy(x_hbm, x_ref, sem.at[1]),
    ]
    for copy in copies:
        copy.start()
    wide_ref[...] = jnp.zeros_like(wide_ref)
    copies[0].wait()
    for out in range(2):
        for dy in range(3):
            for dx in range(3):
                start = ((dy + out) * 3 + dx) * C
                wide_ref[start : start + C, out * C : (out + 1) * C] = w_ref[dy, dx]
    copies[1].wait()
    for f in range(2):
        turn_ref[f] = x_ref[f].reshape(1024, C).T


def forward_kernel(
    x_ref, near_ref, far_ref, wide_ref, turn_ref, slope_ref, act_ref, xt_ref, at_ref, rows_ref
):
    sort_sides(lax.axis_index("core") == 1, near_ref, far_ref, rows_ref.at[:, 0], rows_ref.at[:, 9])
    rows_ref[:, 1:9] = x_ref[...]
    for f in range(2):
        x = rows_ref[f].reshape(1280, C)
        xt_ref[f, :, :128] = rows_ref[f, 0].T
        xt_ref[f, :, 128:1152] = turn_ref[f]
        xt_ref[f, :, 1152:] = rows_ref[f, 9].T
        pre = mm(row_pairs(jnp.concatenate(columns(x), axis=1)), wide_ref[...])
        sig = 1.0 / (1.0 + jnp.exp(-pre))
        act = (pre * sig).astype(BF16)
        slope = sig * (1.0 + pre * (1.0 - sig))
        for out in range(2):
            part = slice(out * C, (out + 1) * C)
            act_ref[f, :, out] = act[:, part].reshape(4, 128, C)
            slope_ref[f, :, out] = slope[:, part].reshape(4, 128, C)
        at_ref[f] = act_ref[f].reshape(1024, C).T


def ahead_kernel(x_ref, act_ref, wt_ref, wd_ref, to_near_ref, to_far_ref):
    zero = jnp.zeros((C, C), BF16)
    a0, a1 = act_ref[0].reshape(1024, C), act_ref[1].reshape(1024, C)
    w_time = jnp.concatenate(
        [
            jnp.concatenate([wt_ref[0], zero], axis=1),
            jnp.concatenate([wt_ref[1], wt_ref[0]], axis=1),
        ],
        axis=0,
    )
    mixed = mm(jnp.concatenate([a0, a1], axis=1), w_time)
    last = (x_ref[1].reshape(1024, C).astype(F32) + mixed[:, :C]).astype(BF16)
    both = jnp.concatenate([last, mixed[:, C:].astype(BF16)], axis=1)
    ahead = mm(both, jnp.concatenate([wd_ref[0], wd_ref[1]], axis=0)).astype(BF16)
    odd = lax.axis_index("yl") == 1

    @pl.when(odd)
    def _():
        to_near_ref[...] = a0.reshape(8, 128, C)
        to_far_ref[...] = ahead.reshape(8, 128, C)

    @pl.when(jnp.logical_not(odd))
    def _():
        to_near_ref[...] = ahead.reshape(8, 128, C)
        to_far_ref[...] = a0.reshape(8, 128, C)


def grads_kernel(
    slope_ref, xt_ref, at_ref, cot_ref, near_ref, far_ref, wt_ref, wd_ref,
    gpre_ref, to_far_ref, send_ref, keep_ref, mats_ref, before_ref, after_ref,
):
    first = frame_index() == 0
    core = lax.axis_index("core")
    sort_sides(lax.axis_index("yl") == 1, near_ref, far_ref, before_ref, after_ref)
    cot, before, after = (r[...].reshape(1024, C) for r in (cot_ref, before_ref, after_ref))
    zero = jnp.zeros((C, C), BF16)
    w_pair = jnp.concatenate(
        [
            jnp.concatenate([wd_ref[2], wd_ref[0]], axis=1),
            jnp.concatenate([zero, wd_ref[1]], axis=1),
        ],
        axis=0,
    )
    low = mm_nt(jnp.concatenate([before, cot], axis=1), w_pair).astype(BF16)
    high = mm_nt(jnp.concatenate([cot, after], axis=1), w_pair).astype(BF16)
    g_m1 = jnp.where(first, jnp.zeros_like(low[:, :C]), low[:, :C])
    g_0, g_1, g_2 = low[:, C:], high[:, :C], high[:, C:]
    w_time = jnp.concatenate(
        [
            jnp.concatenate([wt_ref[2], wt_ref[1], wt_ref[0], zero], axis=1),
            jnp.concatenate([zero, wt_ref[2], wt_ref[1], wt_ref[0]], axis=1),
        ],
        axis=0,
    )
    g_act = mm_nt(jnp.concatenate([g_m1, g_0, g_1, g_2], axis=1), w_time)
    spatial = None
    for f in range(2):
        gp = (g_act[:, f * C : (f + 1) * C] * slope_ref[f].reshape(1024, C)).astype(BF16)
        gpre_ref[f] = gp.reshape(8, 128, C)
        behind, here, ahead = columns(gp)
        shifted = jnp.concatenate([ahead, here, behind], axis=1)
        xt = jnp.concatenate([xt_ref[f, :, dy * 128 : dy * 128 + 1024] for dy in range(3)], axis=0)
        term = mm(xt, shifted)
        spatial = term if spatial is None else spatial + term
    row = 7 * (1 - core)
    for f in range(2):
        send_ref[15 + 2 * f : 17 + 2 * f] = gpre_ref[f, row].reshape(2, 64, C)
        to_far_ref[f] = gpre_ref[f, 7 - row]
    for dy in range(3):
        for dx in range(3):
            mats_ref[dy * 3 + dx] = spatial[dy * C : (dy + 1) * C, dx * C : (dx + 1) * C].reshape(2, 64, C)
    a0, a1 = at_ref[0], at_ref[1]
    x0, x1 = xt_ref[0, :, 128:1152], xt_ref[1, :, 128:1152]
    time = mm(a0, jnp.concatenate([g_1, g_0, g_m1], axis=1))
    time = time + mm(a1, jnp.concatenate([g_2, g_1, g_0], axis=1))
    for k in range(3):
        mats_ref[9 + k] = time[:, k * C : (k + 1) * C].reshape(2, 64, C)
    both = mm(
        jnp.concatenate([a0, a1, x0, x1], axis=0), jnp.concatenate([cot, after], axis=1)
    )
    tail = mm(a0, before)
    m_0, m_1 = both[0:128, :C], both[128:256, :C]
    m_m2, m_m1 = both[0:128, C:], both[128:256, C:]
    skip = jnp.where(first, jnp.zeros_like(m_0), m_0)
    kinds = (
        (both[384:512, C:], (m_m2, m_m1, skip)),
        (both[256:384, :C], (m_m1, m_0, m_1)),
        (both[384:512, :C], (m_0, m_1, tail)),
    )
    for k, (base, terms) in enumerate(kinds):
        total = base
        for tap, m in enumerate(terms):
            top = m.astype(BF16)
            rest = (m - top.astype(F32)).astype(BF16)
            total = total + mm_tn(wt_ref[tap], top) + mm_tn(wt_ref[tap], rest)
        mats_ref[12 + k] = total.reshape(2, 64, C)
    send_ref[:15] = mats_ref[:, 1 - core].astype(BF16)
    keep_ref[...] = mats_ref[:, core]


def merge_kernel(keep_ref, got_ref, out_ref):
    out_ref[:15] = (keep_ref[...] + got_ref[:15].astype(F32)).astype(BF16)
    out_ref[15] = jnp.zeros((64, C), BF16)


def down_kernel(x_ref, act_ref, near_ref, far_ref, wt_ref, wd_ref, out_ref, ahead_ref, after_ref):
    sort_sides(lax.axis_index("yl") == 1, near_ref, far_ref, ahead_ref, after_ref)
    zero = jnp.zeros((C, C), BF16)
    first = jnp.where(frame_index() == 0, zero, wt_ref[2])
    w_time = jnp.concatenate(
        [
            jnp.concatenate([first, wt_ref[1], wt_ref[0]], axis=1),
            jnp.concatenate([zero, wt_ref[2], wt_ref[1]], axis=1),
            jnp.concatenate([zero, zero, wt_ref[2]], axis=1),
        ],
        axis=0,
    )
    parts = [act_ref[0], act_ref[1], after_ref[...]]
    mixed = mm(jnp.concatenate([p.reshape(1024, C) for p in parts], axis=1), w_time)
    resid = [mixed[:, :C].astype(BF16)]
    for f in range(2):
        total = x_ref[f].astype(F32).reshape(1024, C) + mixed[:, (f + 1) * C : (f + 2) * C]
        resid.append(total.astype(BF16))
    weights = jnp.concatenate([wd_ref[0], wd_ref[1], wd_ref[2]], axis=0)
    down = mm(jnp.concatenate(resid, axis=1), weights)
    down = down + ahead_ref[...].reshape(1024, C).astype(F32)
    out_ref[...] = down.astype(BF16).reshape(8, 128, C)


def features_kernel(
    gpre_ref, sent_ref, g_far_ref, cot_ref, near_ref, far_ref, w_ref, wd_ref,
    out_ref, wide_ref, rows_ref, before_ref, after_ref,
):
    wide_ref[...] = jnp.zeros_like(wide_ref)
    for out in range(2):
        for dy in range(3):
            for dx in range(3):
                start = ((dy + out) * 3 + dx) * C
                wide_ref[out * C : (out + 1) * C, start : start + C] = w_ref[2 - dy, 2 - dx]
    zero = jnp.zeros((C, C), BF16)
    w_pair = jnp.concatenate(
        [
            jnp.concatenate([wd_ref[1], zero], axis=1),
            jnp.concatenate([wd_ref[2], wd_ref[0]], axis=1),
        ],
        axis=0,
    )
    sort_sides(lax.axis_index("yl") == 1, near_ref, far_ref, before_ref, after_ref)
    for f in range(2):
        near_ref_f = sent_ref.at[15 + 2 * f : 17 + 2 * f]
        sort_rows(near_ref_f, g_far_ref.at[f], rows_ref.at[f, 0], rows_ref.at[f, 9])
    rows_ref[:, 1:9] = gpre_ref[...]
    cot, after = (r[...].reshape(1024, C) for r in (cot_ref, after_ref))
    resid = mm_nt(jnp.concatenate([cot, after], axis=1), w_pair)
    for f in range(2):
        g = rows_ref[f].reshape(1280, C)
        conv = mm_nt(row_pairs(jnp.concatenate(columns(g), axis=1)), wide_ref[...])
        base = resid[:, f * C : (f + 1) * C].reshape(4, 2, 128, C)
        for out in range(2):
            part = conv[:, out * C : (out + 1) * C].reshape(4, 128, C)
            out_ref[f, :, out] = (base[:, out] + part).astype(BF16)


VMEM = pl.BlockSpec(memory_space=pltpu.VMEM)


def call(kernel, outs, args, taps, scratch=()):
    return pl.pallas_call(
        kernel,
        out_shape=[jax.ShapeDtypeStruct(s, d) for s, d in outs],
        in_specs=[VMEM] * len(args),
        out_specs=[VMEM] * len(outs),
        scratch_shapes=list(scratch),
        compiler_params=pltpu.CompilerParams(vmem_limit_bytes=24 * 1024 * 1024),
        cost_estimate=pl.CostEstimate(
            flops=int(taps * 2048 * C * C * 2), bytes_accessed=4_000_000, transcendentals=0
        ),
    )(*args)


def gather_kernel(mine_ref, other_ref, spatial_ref, time_ref, down_ref):
    mine = lax.axis_index("core") == 0
    low = jnp.where(mine, mine_ref[...], other_ref[...]).astype(F32)
    high = jnp.where(mine, other_ref[...], mine_ref[...]).astype(F32)
    for first, ref in ((0, spatial_ref), (9, time_ref), (12, down_ref)):
        count = ref.shape[0]
        ref[:, :64] = low[first : first + count]
        ref[:, 64:] = high[first : first + count]


def exchange(x, axis, order):
    groups = [list(order)]
    return lax.all_to_all(x, axis, 0, 0, axis_index_groups=groups, tiled=True)


def swap(x, axis, mask):
    return lax.ppermute(x, axis, [(i, i ^ mask) for i in range(lax.axis_size(axis))])


def swap_far(x, axis):
    count = lax.axis_size(axis)
    pairs = [(i, i + 1) for i in range(1, count - 1, 2)]
    return lax.ppermute(x, axis, pairs + [(b, a) for a, b in pairs])


def per_device(features, w_spatial, w_temporal, w_down, cotangent):
    time, rows = ("z", "yl"), ("x", "core")
    x, cot = features[0], cotangent[0, 0]
    frame, edge = ((8, 128, C), BF16), ((2, 128, C), BF16)
    frame_scratch, rows_scratch = pltpu.VMEM(*frame), pltpu.VMEM((2, 10, 128, C), BF16)
    cot_near, cot_far = swap(cot, time, 1), swap_far(cot, time)
    low, high = lax.optimization_barrier((x[:, 0], x[:, 7]))
    to_near, to_far = call(pick_kernel, [edge, edge], (low, high), 0)
    x_near, x_far = swap(to_near, rows, 1), swap_far(to_far, rows)
    source, _ = lax.optimization_barrier((x, to_near))
    here, wide, turn = pl.pallas_call(
        prepare_kernel,
        out_shape=[jax.ShapeDtypeStruct((2, 8, 128, C), BF16), jax.ShapeDtypeStruct((12 * C, 2 * C), BF16), jax.ShapeDtypeStruct((2, C, 1024), BF16)],
        in_specs=[pl.BlockSpec(memory_space=pl.ANY)] * 2,
        out_specs=[VMEM] * 3,
        scratch_shapes=[pltpu.VMEM((3, 3, C, C), BF16), pltpu.SemaphoreType.DMA((2,))],
        compiler_params=pltpu.CompilerParams(vmem_limit_bytes=24 * 1024 * 1024),
    )(source, w_spatial)
    slope, act, xt, at = call(
        forward_kernel,
        [((2, 4, 2, 128, C), F32), ((2, 4, 2, 128, C), BF16), ((2, C, 1280), BF16), ((2, C, 1024), BF16)],
        (here, x_near, x_far, wide, turn), 9,
        scratch=[rows_scratch],
    )
    gpre, to_far, send, keep = call(
        grads_kernel,
        [((2, 8, 128, C), BF16), edge, ((19, 64, C), BF16), ((15, 64, C), F32)],
        (slope, xt, at, cot, cot_near, cot_far, w_temporal, w_down), 21,
        scratch=[pltpu.VMEM((15, 2, 64, C), F32), frame_scratch, frame_scratch],
    )
    near = swap(send, "core", 1)
    (half,) = call(merge_kernel, [((16, 64, C), BF16)], (keep, near), 0)
    _, recent = lax.optimization_barrier((send, act))
    to_t_near, to_t_far = call(ahead_kernel, [frame, frame], (here, recent, w_temporal, w_down), 2)
    half, to_t_near, to_t_far = lax.optimization_barrier((half, to_t_near, to_t_far))
    got = exchange(half, PLANE, range(15, -1, -1))
    got, to_far, to_t_near, to_t_far = lax.optimization_barrier((got, to_far, to_t_near, to_t_far))
    total = jnp.sum(got.astype(F32), axis=0)
    t_near, t_far = swap(to_t_near, time, 1), swap_far(to_t_far, time)
    g_far = swap_far(to_far, rows)
    column = jnp.broadcast_to(total.astype(BF16), (8, 64, C))
    column = exchange(column, "z", [4, 3, 5, 2, 6, 1, 7, 0])
    column, g_far = lax.optimization_barrier((column, g_far))
    total = jnp.sum(column.astype(F32), axis=0)
    out = jnp.broadcast_to(total.astype(BF16), (16, 64, C))
    out = exchange(out, PLANE, range(15, -1, -1))
    (down,) = call(
        down_kernel, [frame], (x, act.reshape(2, 8, 128, C), t_near, t_far, w_temporal, w_down), 5,
        scratch=[frame_scratch, frame_scratch],
    )
    (grad_features,) = call(
        features_kernel, [((2, 4, 2, 128, C), BF16)],
        (gpre, near, g_far, cot, cot_near, cot_far, w_spatial, w_down), 11,
        scratch=[pltpu.VMEM((2 * C, 12 * C), BF16), rows_scratch, frame_scratch, frame_scratch],
    )
    out, down, grad_features = lax.optimization_barrier((out, down, grad_features))
    grads = call(
        gather_kernel, [((n, C, C), F32) for n in (9, 3, 3)], (out, swap(out, "core", 1)), 0,
    )
    return (
        down[None, None],
        grad_features.reshape(1, 2, 8, 128, C),
        grads[0].reshape(3, 3, C, C),
        grads[1],
        grads[2],
    )


def solution(mesh):
    fine = Mesh(mesh.devices.reshape(2, 8, 2, 4, 2), ("yh", "z", "yl", "x", "core"))
    block = P("yh", ("z", "yl"), ("x", "core"), None, None)
    return jax.shard_map(
        per_device,
        mesh=fine,
        in_specs=(block, P(), P(), P(), block),
        out_specs=(block, block, P(), P(), P()),
        check_vma=False,
    )
```

```python
import jax
import jax.numpy as jnp
from jax import lax
from jax.experimental import pallas as pl
from jax.experimental.pallas import tpu as pltpu
from jax.sharding import Mesh, PartitionSpec as P

F32, BF16 = jnp.float32, jnp.bfloat16
C = 128
PLANE = ("yh", "yl", "x")


def mm(a, b):
    return lax.dot_general(a, b, (((1,), (0,)), ((), ())), preferred_element_type=F32)


def mm_nt(a, b):
    return lax.dot_general(a, b, (((1,), (1,)), ((), ())), preferred_element_type=F32)


def mm_tn(a, b):
    return lax.dot_general(a, b, (((0,), (0,)), ((), ())), preferred_element_type=F32)


def columns(x):
    wide = x.astype(F32)
    count = wide.shape[0]
    col = lax.broadcasted_iota(jnp.int32, wide.shape, 0) % 128
    before = jnp.where(col == 0, 0.0, pltpu.roll(wide, 1, 0)).astype(BF16)
    after = jnp.where(col == 127, 0.0, pltpu.roll(wide, count - 1, 0)).astype(BF16)
    return before, x, after


def row_pairs(cat):
    depth = cat.shape[1]
    rows = cat.reshape(5, 2, 128, depth)
    even, odd = rows[:, 0], rows[:, 1]
    parts = [even[0:4], odd[0:4], even[1:5], odd[1:5]]
    return jnp.concatenate([p.reshape(512, depth) for p in parts], axis=1)


def frame_index():
    return lax.axis_index("z") * 2 + lax.axis_index("yl")


def sort_sides(odd, near_ref, far_ref, before_ref, after_ref):
    @pl.when(odd)
    def _():
        before_ref[...] = near_ref[...]
        after_ref[...] = far_ref[...]

    @pl.when(jnp.logical_not(odd))
    def _():
        before_ref[...] = far_ref[...]
        after_ref[...] = near_ref[...]


def sort_rows(near_ref, far_ref, low_ref, high_ref):
    @pl.when(lax.axis_index("core") == 1)
    def _():
        low_ref[...] = near_ref[...].reshape(128, C)
        high_ref[...] = far_ref[...]

    @pl.when(lax.axis_index("core") == 0)
    def _():
        low_ref[...] = far_ref[...]
        high_ref[...] = near_ref[...].reshape(128, C)


def pick_kernel(low_ref, high_ref, near_ref, far_ref):
    sort_sides(lax.axis_index("core") == 1, low_ref, high_ref, near_ref, far_ref)


def prepare_kernel(x_hbm, w_hbm, x_ref, wide_ref, turn_ref, w_ref, sem):
    copies = [
        pltpu.make_async_copy(w_hbm, w_ref, sem.at[0]),
        pltpu.make_async_copy(x_hbm, x_ref, sem.at[1]),
    ]
    for copy in copies:
        copy.start()
    wide_ref[...] = jnp.zeros_like(wide_ref)
    copies[0].wait()
    for out in range(2):
        for dy in range(3):
            for dx in range(3):
                start = ((dy + out) * 3 + dx) * C
                wide_ref[start : start + C, out * C : (out + 1) * C] = w_ref[dy, dx]
    copies[1].wait()
    for f in range(2):
        turn_ref[f] = x_ref[f].reshape(1024, C).T


def forward_kernel(
    x_ref, near_ref, far_ref, wide_ref, turn_ref, slope_ref, act_ref, xt_ref, at_ref, rows_ref
):
    sort_sides(lax.axis_index("core") == 1, near_ref, far_ref, rows_ref.at[:, 0], rows_ref.at[:, 9])
    rows_ref[:, 1:9] = x_ref[...]
    for f in range(2):
        x = rows_ref[f].reshape(1280, C)
        xt_ref[f, :, :128] = rows_ref[f, 0].T
        xt_ref[f, :, 128:1152] = turn_ref[f]
        xt_ref[f, :, 1152:] = rows_ref[f, 9].T
        pre = mm(row_pairs(jnp.concatenate(columns(x), axis=1)), wide_ref[...])
        sig = 1.0 / (1.0 + jnp.exp(-pre))
        act = (pre * sig).astype(BF16)
        slope = sig * (1.0 + pre * (1.0 - sig))
        for out in range(2):
            part = slice(out * C, (out + 1) * C)
            act_ref[f, :, out] = act[:, part].reshape(4, 128, C)
            slope_ref[f, :, out] = slope[:, part].reshape(4, 128, C)
        at_ref[f] = act_ref[f].reshape(1024, C).T


def ahead_kernel(x_ref, act_ref, wt_ref, wd_ref, to_near_ref, to_far_ref):
    zero = jnp.zeros((C, C), BF16)
    a0, a1 = act_ref[0].reshape(1024, C), act_ref[1].reshape(1024, C)
    w_time = jnp.concatenate(
        [
            jnp.concatenate([wt_ref[0], zero], axis=1),
            jnp.concatenate([wt_ref[1], wt_ref[0]], axis=1),
        ],
        axis=0,
    )
    mixed = mm(jnp.concatenate([a0, a1], axis=1), w_time)
    last = (x_ref[1].reshape(1024, C).astype(F32) + mixed[:, :C]).astype(BF16)
    both = jnp.concatenate([last, mixed[:, C:].astype(BF16)], axis=1)
    ahead = mm(both, jnp.concatenate([wd_ref[0], wd_ref[1]], axis=0)).astype(BF16)
    odd = lax.axis_index("yl") == 1

    @pl.when(odd)
    def _():
        to_near_ref[...] = a0.reshape(8, 128, C)
        to_far_ref[...] = ahead.reshape(8, 128, C)

    @pl.when(jnp.logical_not(odd))
    def _():
        to_near_ref[...] = ahead.reshape(8, 128, C)
        to_far_ref[...] = a0.reshape(8, 128, C)


def grads_kernel(
    slope_ref, xt_ref, at_ref, cot_ref, near_ref, far_ref, wt_ref, wd_ref,
    gpre_ref, to_far_ref, send_ref, keep_ref, mats_ref, before_ref, after_ref,
):
    first = frame_index() == 0
    core = lax.axis_index("core")
    sort_sides(lax.axis_index("yl") == 1, near_ref, far_ref, before_ref, after_ref)
    cot, before, after = (r[...].reshape(1024, C) for r in (cot_ref, before_ref, after_ref))
    zero = jnp.zeros((C, C), BF16)
    w_pair = jnp.concatenate(
        [
            jnp.concatenate([wd_ref[2], wd_ref[0]], axis=1),
            jnp.concatenate([zero, wd_ref[1]], axis=1),
        ],
        axis=0,
    )
    low = mm_nt(jnp.concatenate([before, cot], axis=1), w_pair).astype(BF16)
    high = mm_nt(jnp.concatenate([cot, after], axis=1), w_pair).astype(BF16)
    g_m1 = jnp.where(first, jnp.zeros_like(low[:, :C]), low[:, :C])
    g_0, g_1, g_2 = low[:, C:], high[:, :C], high[:, C:]
    w_time = jnp.concatenate(
        [
            jnp.concatenate([wt_ref[2], wt_ref[1], wt_ref[0], zero], axis=1),
            jnp.concatenate([zero, wt_ref[2], wt_ref[1], wt_ref[0]], axis=1),
        ],
        axis=0,
    )
    g_act = mm_nt(jnp.concatenate([g_m1, g_0, g_1, g_2], axis=1), w_time)
    spatial = None
    for f in range(2):
        gp = (g_act[:, f * C : (f + 1) * C] * slope_ref[f].reshape(1024, C)).astype(BF16)
        gpre_ref[f] = gp.reshape(8, 128, C)
        behind, here, ahead = columns(gp)
        shifted = jnp.concatenate([ahead, here, behind], axis=1)
        xt = jnp.concatenate([xt_ref[f, :, dy * 128 : dy * 128 + 1024] for dy in range(3)], axis=0)
        term = mm(xt, shifted)
        spatial = term if spatial is None else spatial + term
    row = 7 * (1 - core)
    for f in range(2):
        send_ref[15 + 2 * f : 17 + 2 * f] = gpre_ref[f, row].reshape(2, 64, C)
        to_far_ref[f] = gpre_ref[f, 7 - row]
    for dy in range(3):
        for dx in range(3):
            mats_ref[dy * 3 + dx] = spatial[dy * C : (dy + 1) * C, dx * C : (dx + 1) * C].reshape(2, 64, C)
    a0, a1 = at_ref[0], at_ref[1]
    x0, x1 = xt_ref[0, :, 128:1152], xt_ref[1, :, 128:1152]
    time = mm(a0, jnp.concatenate([g_1, g_0, g_m1], axis=1))
    time = time + mm(a1, jnp.concatenate([g_2, g_1, g_0], axis=1))
    for k in range(3):
        mats_ref[9 + k] = time[:, k * C : (k + 1) * C].reshape(2, 64, C)
    both = mm(
        jnp.concatenate([a0, a1, x0, x1], axis=0), jnp.concatenate([cot, after], axis=1)
    )
    tail = mm(a0, before)
    m_0, m_1 = both[0:128, :C], both[128:256, :C]
    m_m2, m_m1 = both[0:128, C:], both[128:256, C:]
    skip = jnp.where(first, jnp.zeros_like(m_0), m_0)
    kinds = (
        (both[384:512, C:], (m_m2, m_m1, skip)),
        (both[256:384, :C], (m_m1, m_0, m_1)),
        (both[384:512, :C], (m_0, m_1, tail)),
    )
    for k, (base, terms) in enumerate(kinds):
        total = base
        for tap, m in enumerate(terms):
            top = m.astype(BF16)
            rest = (m - top.astype(F32)).astype(BF16)
            total = total + mm_tn(wt_ref[tap], top) + mm_tn(wt_ref[tap], rest)
        mats_ref[12 + k] = total.reshape(2, 64, C)
    send_ref[:15] = mats_ref[:, 1 - core].astype(BF16)
    keep_ref[...] = mats_ref[:, core]


def merge_kernel(keep_ref, got_ref, out_ref):
    out_ref[:15] = (keep_ref[...] + got_ref[:15].astype(F32)).astype(BF16)
    out_ref[15] = jnp.zeros((64, C), BF16)


def down_kernel(x_ref, act_ref, near_ref, far_ref, wt_ref, wd_ref, out_ref, ahead_ref, after_ref):
    sort_sides(lax.axis_index("yl") == 1, near_ref, far_ref, ahead_ref, after_ref)
    zero = jnp.zeros((C, C), BF16)
    first = jnp.where(frame_index() == 0, zero, wt_ref[2])
    w_time = jnp.concatenate(
        [
            jnp.concatenate([first, wt_ref[1], wt_ref[0]], axis=1),
            jnp.concatenate([zero, wt_ref[2], wt_ref[1]], axis=1),
            jnp.concatenate([zero, zero, wt_ref[2]], axis=1),
        ],
        axis=0,
    )
    parts = [act_ref[0], act_ref[1], after_ref[...]]
    mixed = mm(jnp.concatenate([p.reshape(1024, C) for p in parts], axis=1), w_time)
    resid = [mixed[:, :C].astype(BF16)]
    for f in range(2):
        total = x_ref[f].astype(F32).reshape(1024, C) + mixed[:, (f + 1) * C : (f + 2) * C]
        resid.append(total.astype(BF16))
    weights = jnp.concatenate([wd_ref[0], wd_ref[1], wd_ref[2]], axis=0)
    down = mm(jnp.concatenate(resid, axis=1), weights)
    down = down + ahead_ref[...].reshape(1024, C).astype(F32)
    out_ref[...] = down.astype(BF16).reshape(8, 128, C)


def features_kernel(
    gpre_ref, sent_ref, g_far_ref, cot_ref, near_ref, far_ref, w_ref, wd_ref,
    out_ref, wide_ref, rows_ref, before_ref, after_ref,
):
    wide_ref[...] = jnp.zeros_like(wide_ref)
    for out in range(2):
        for dy in range(3):
            for dx in range(3):
                start = ((dy + out) * 3 + dx) * C
                wide_ref[out * C : (out + 1) * C, start : start + C] = w_ref[2 - dy, 2 - dx]
    zero = jnp.zeros((C, C), BF16)
    w_pair = jnp.concatenate(
        [
            jnp.concatenate([wd_ref[1], zero], axis=1),
            jnp.concatenate([wd_ref[2], wd_ref[0]], axis=1),
        ],
        axis=0,
    )
    sort_sides(lax.axis_index("yl") == 1, near_ref, far_ref, before_ref, after_ref)
    for f in range(2):
        near_ref_f = sent_ref.at[15 + 2 * f : 17 + 2 * f]
        sort_rows(near_ref_f, g_far_ref.at[f], rows_ref.at[f, 0], rows_ref.at[f, 9])
    rows_ref[:, 1:9] = gpre_ref[...]
    cot, after = (r[...].reshape(1024, C) for r in (cot_ref, after_ref))
    resid = mm_nt(jnp.concatenate([cot, after], axis=1), w_pair)
    for f in range(2):
        g = rows_ref[f].reshape(1280, C)
        conv = mm_nt(row_pairs(jnp.concatenate(columns(g), axis=1)), wide_ref[...])
        base = resid[:, f * C : (f + 1) * C].reshape(4, 2, 128, C)
        for out in range(2):
            part = conv[:, out * C : (out + 1) * C].reshape(4, 128, C)
            out_ref[f, :, out] = (base[:, out] + part).astype(BF16)


VMEM = pl.BlockSpec(memory_space=pltpu.VMEM)


def call(kernel, outs, args, taps, scratch=()):
    return pl.pallas_call(
        kernel,
        out_shape=[jax.ShapeDtypeStruct(s, d) for s, d in outs],
        in_specs=[VMEM] * len(args),
        out_specs=[VMEM] * len(outs),
        scratch_shapes=list(scratch),
        compiler_params=pltpu.CompilerParams(vmem_limit_bytes=24 * 1024 * 1024),
        cost_estimate=pl.CostEstimate(
            flops=int(taps * 2048 * C * C * 2), bytes_accessed=4_000_000, transcendentals=0
        ),
    )(*args)


def write_half(side, half_ref, outs, wide_ref, sem):
    wide_ref[...] = half_ref[:15].astype(F32)
    rows = pl.ds(pl.multiple_of(side * 64, 64), 64)
    copies = []
    for i, (first, out) in enumerate(zip((0, 9, 12), outs)):
        count = out.shape[0]
        copies.append(
            pltpu.make_async_copy(wide_ref.at[first : first + count], out.at[:, rows], sem.at[i])
        )
    for copy in copies:
        copy.start()
    for copy in copies:
        copy.wait()


def own_half_kernel(half_ref, spatial_hbm, time_hbm, down_hbm, wide_ref, sem):
    outs = (spatial_hbm, time_hbm, down_hbm)
    write_half(lax.axis_index("core"), half_ref, outs, wide_ref, sem)


def other_half_kernel(half_ref, a, b, c, spatial_hbm, time_hbm, down_hbm, wide_ref, sem):
    outs = (spatial_hbm, time_hbm, down_hbm)
    write_half(1 - lax.axis_index("core"), half_ref, outs, wide_ref, sem)


def exchange(x, axis, order):
    groups = [list(order)]
    return lax.all_to_all(x, axis, 0, 0, axis_index_groups=groups, tiled=True)


def swap(x, axis, mask):
    return lax.ppermute(x, axis, [(i, i ^ mask) for i in range(lax.axis_size(axis))])


def swap_far(x, axis):
    count = lax.axis_size(axis)
    pairs = [(i, i + 1) for i in range(1, count - 1, 2)]
    return lax.ppermute(x, axis, pairs + [(b, a) for a, b in pairs])


def per_device(features, w_spatial, w_temporal, w_down, cotangent):
    time, rows = ("z", "yl"), ("x", "core")
    x, cot = features[0], cotangent[0, 0]
    frame, edge = ((8, 128, C), BF16), ((2, 128, C), BF16)
    frame_scratch, rows_scratch = pltpu.VMEM(*frame), pltpu.VMEM((2, 10, 128, C), BF16)
    cot_near, cot_far = swap(cot, time, 1), swap_far(cot, time)
    low, high = lax.optimization_barrier((x[:, 0], x[:, 7]))
    to_near, to_far = call(pick_kernel, [edge, edge], (low, high), 0)
    x_near, x_far = swap(to_near, rows, 1), swap_far(to_far, rows)
    source, _ = lax.optimization_barrier((x, to_near))
    here, wide, turn = pl.pallas_call(
        prepare_kernel,
        out_shape=[jax.ShapeDtypeStruct((2, 8, 128, C), BF16), jax.ShapeDtypeStruct((12 * C, 2 * C), BF16), jax.ShapeDtypeStruct((2, C, 1024), BF16)],
        in_specs=[pl.BlockSpec(memory_space=pl.ANY)] * 2,
        out_specs=[VMEM] * 3,
        scratch_shapes=[pltpu.VMEM((3, 3, C, C), BF16), pltpu.SemaphoreType.DMA((2,))],
        compiler_params=pltpu.CompilerParams(vmem_limit_bytes=24 * 1024 * 1024),
    )(source, w_spatial)
    slope, act, xt, at = call(
        forward_kernel,
        [((2, 4, 2, 128, C), F32), ((2, 4, 2, 128, C), BF16), ((2, C, 1280), BF16), ((2, C, 1024), BF16)],
        (here, x_near, x_far, wide, turn), 9,
        scratch=[rows_scratch],
    )
    gpre, to_far, send, keep = call(
        grads_kernel,
        [((2, 8, 128, C), BF16), edge, ((19, 64, C), BF16), ((15, 64, C), F32)],
        (slope, xt, at, cot, cot_near, cot_far, w_temporal, w_down), 21,
        scratch=[pltpu.VMEM((15, 2, 64, C), F32), frame_scratch, frame_scratch],
    )
    near = swap(send, "core", 1)
    (half,) = call(merge_kernel, [((16, 64, C), BF16)], (keep, near), 0)
    _, recent = lax.optimization_barrier((send, act))
    to_t_near, to_t_far = call(ahead_kernel, [frame, frame], (here, recent, w_temporal, w_down), 2)
    half, to_t_near, to_t_far = lax.optimization_barrier((half, to_t_near, to_t_far))
    got = exchange(half, PLANE, range(15, -1, -1))
    got, to_far, to_t_near, to_t_far = lax.optimization_barrier((got, to_far, to_t_near, to_t_far))
    total = jnp.sum(got.astype(F32), axis=0)
    t_near, t_far = swap(to_t_near, time, 1), swap_far(to_t_far, time)
    g_far = swap_far(to_far, rows)
    column = jnp.broadcast_to(total.astype(BF16), (8, 64, C))
    column = exchange(column, "z", [4, 3, 5, 2, 6, 1, 0, 7])
    column, g_far = lax.optimization_barrier((column, g_far))
    total = jnp.sum(column.astype(F32), axis=0)
    out = jnp.broadcast_to(total.astype(BF16), (16, 64, C))
    out = exchange(out, PLANE, range(15, -1, -1))
    (down,) = call(
        down_kernel, [frame], (x, act.reshape(2, 8, 128, C), t_near, t_far, w_temporal, w_down), 5,
        scratch=[frame_scratch, frame_scratch],
    )
    (grad_features,) = call(
        features_kernel, [((2, 4, 2, 128, C), BF16)],
        (gpre, near, g_far, cot, cot_near, cot_far, w_spatial, w_down), 11,
        scratch=[pltpu.VMEM((2 * C, 12 * C), BF16), rows_scratch, frame_scratch, frame_scratch],
    )
    out, down, grad_features = lax.optimization_barrier((out, down, grad_features))
    anywhere = pl.BlockSpec(memory_space=pl.ANY)
    shared = dict(
        out_shape=[jax.ShapeDtypeStruct((n, C, C), F32) for n in (9, 3, 3)],
        out_specs=[anywhere] * 3,
        scratch_shapes=[pltpu.VMEM((15, 64, C), F32), pltpu.SemaphoreType.DMA((3,))],
        compiler_params=pltpu.CompilerParams(vmem_limit_bytes=24 * 1024 * 1024),
    )
    other = swap(out, "core", 1)
    grads = pl.pallas_call(own_half_kernel, in_specs=[VMEM], **shared)(out)
    grads = pl.pallas_call(
        other_half_kernel, in_specs=[VMEM] + [anywhere] * 3,
        input_output_aliases={1: 0, 2: 1, 3: 2}, **shared,
    )(other, *grads)
    return (
        down[None, None],
        grad_features.reshape(1, 2, 8, 128, C),
        grads[0].reshape(3, 3, C, C),
        grads[1],
        grads[2],
    )


def solution(mesh):
    fine = Mesh(mesh.devices.reshape(2, 8, 2, 4, 2), ("yh", "z", "yl", "x", "core"))
    block = P("yh", ("z", "yl"), ("x", "core"), None, None)
    return jax.shard_map(
        per_device,
        mesh=fine,
        in_specs=(block, P(), P(), P(), block),
        out_specs=(block, block, P(), P(), P()),
        check_vma=False,
    )
```
